32 devices in a mesh: groups: 2 (over x), dp: 16 (over z, y, core).
Axes of the slice: x: 2, y: 2, z: 4, core: 2. Of those that a mesh axis runs over, the one named last changes fastest.
Arguments:
- coords: float32 [3, 8192], P(None, ('groups', 'dp')), parts along dimension 1, may hold values from -1 to 1
- forcing: float32 [3, 8192], P(None, ('groups', 'dp')), parts along dimension 1, may hold values from -6 to 6
- bins: int32 [8192], P(('groups', 'dp')), parts along dimension 0, may hold values from 0 to 15
- counts: int32 [32], P(('groups', 'dp')), parts along dimension 0, may hold values from 1 to 255, as said below
- bin_weight: float32 [32], P('groups'), parts along dimension 0, may hold values from 0.3 to 3
- w_in: float32 [6, 1024], P('groups'), parts along dimension 0, may hold values from -6 to 6
- b_in: float32 [2048], P('groups'), parts along dimension 0, may hold values from -3 to 3
- w_mid: bfloat16 [2048, 1024], P('groups'), parts along dimension 0, may hold values from -0.1875 to 0.1875
- b_mid: float32 [2048], P('groups'), parts along dimension 0, may hold values from -2 to 2
- w_out: bfloat16 [2048, 4], P('groups'), parts along dimension 0, may hold values from -0.1875 to 0.1875
- b_out: float32 [8], P('groups'), parts along dimension 0, may hold values from -3 to 3
Outputs:
- update: float32 [2048, 4], P(('groups', 'dp')), parts along dimension 0
- inverse_factor: float32 [2048, 1024], P(('groups', 'dp')), parts along dimension 0
The draws below stay inside these ranges and needn't reach their ends.
There are 2 independent parts, one for each index of `groups`. The reference program is written for one: setup_inputs(seed, part) draws one part's arguments, and reference() takes and returns one part's arrays. A program takes and returns all parts, laid end to end along the dimension named above; each array names one. Nothing has to cross between parts.
Inputs may be any that keep to these rules, and one draw needn't show every extreme that they name: Each dp device has 256 slots of points; the first counts[i] of device i are live. The live points of a device and of the device half the dp axis away number at most 256 together, exactly 256 for some pair.
All inputs are finite; a program needn't handle non-finite values. Where the reference program divides by a largest or mean magnitude, that divisor is 1e-20 or more.
Results may differ from the reference program's by a relative error of at most 0.0034.
Values sent between devices are 32-bit elements; how exact they have to be, the bound alone decides.
A program may use at most 64 MiB of HBM per device.

```python
import math
import jax
import jax.numpy as jnp
from jax import lax

D = 1024
CAP = 256
BINS = 16
ITERS = 6
POINTS = 4096
N_DP = 16


def draw_counts(key, part):
    key = jax.random.fold_in(key, 11)
    half = N_DP // 2
    key_first, key_extra, key_flip = jax.random.split(key, 3)
    first = jax.random.randint(key_first, (half,), 1, CAP, dtype=jnp.int32)
    first = first.at[0].set(CAP - 1)
    extra = jax.random.randint(key_extra, (half,), 0, CAP - first, dtype=jnp.int32)
    extra = extra.at[0].set(0)
    second = CAP - first - extra
    flip = jax.random.randint(key_flip, (half,), 0, 2, dtype=jnp.int32)
    lower = jnp.where(flip == 1, second, first)
    upper = jnp.where(flip == 1, first, second)
    return jnp.concatenate([lower, upper]).astype(jnp.int32)


def draw_coords(key, part):
    key = jax.random.fold_in(key, 23)
    values = jax.random.uniform(key, (3, POINTS), jnp.float32, -1.0, 1.0)
    return jnp.clip(values, -1.0, 1.0).astype(jnp.float32)


def draw_w_in(key, part):
    key = jax.random.fold_in(key, 37)
    values = jnp.clip(3.0 * jax.random.normal(key, (3, D), jnp.float32), -6.0, 6.0)
    return values.astype(jnp.float32)


def plant(values, own_key, low, largest):
    extent = values.shape
    index_at = [jax.random.randint(jax.random.fold_in(own_key, axis), (), 0, extent[axis]) for axis in range(len(extent))]
    values = values.at[tuple(index_at)].set(low)
    longest = extent.index(max(extent))
    index_at[longest] = (index_at[longest] + 1) % extent[longest]
    return values.at[tuple(index_at)].set(largest)


def block_levels(stream_key, dims, cuts, least, top_value):
    level = 1.0
    for axis_at, parts in cuts:
        heights = jax.random.uniform(jax.random.fold_in(jax.random.fold_in(stream_key, 6), axis_at), (parts,), jnp.float32, least / len(cuts), top_value / len(cuts))
        level = level * jnp.repeat(jnp.exp(heights), dims[axis_at] // parts).reshape((-1,) + (1,) * (len(dims) - 1 - axis_at))
    return level


def normal_values(own_key, dims, scale, most, cuts=(), held_as=jnp.bfloat16):
    values = jax.random.normal(own_key, dims, jnp.float32) * scale
    if len(cuts) > 0:
        values = block_levels(own_key, dims, cuts, -0.22, 0.18) * values
    return jnp.clip(values, min=-most, max=most).astype(held_as)


def setup_inputs(seed: int = 0, part: int = 0) -> dict:
    key_of = jax.random.split(jax.random.key(seed), 12)
    part_splits = jax.random.split(jax.random.fold_in(key_of[11], part), 12)
    return {
        "coords": draw_coords(jax.random.fold_in(jax.random.fold_in(key_of[11], part), 71), part),
        "forcing": normal_values(part_splits[1], (3, POINTS), 1.0, 6.0, ((1, 16),), jnp.float32),
        "bins": plant(jax.random.randint(part_splits[2], (POINTS,), 0, BINS), jax.random.fold_in(part_splits[2], 1), 0, BINS - 1).astype(jnp.int32),
        "counts": draw_counts(jax.random.fold_in(jax.random.fold_in(key_of[11], part), 71), part),
        "bin_weight": jnp.clip(jnp.exp(jax.random.uniform(part_splits[4], (BINS,), jnp.float32, math.log(0.3), math.log(3.0))), 0.3, 3.0),
        "w_in": draw_w_in(jax.random.fold_in(jax.random.fold_in(key_of[11], part), 71), part),
        "b_in": normal_values(part_splits[6], (D,), 0.5, 3.0, (), jnp.float32),
        "w_mid": normal_values(part_splits[7], (D, D), D ** -0.5, 0.1875),
        "b_mid": normal_values(part_splits[8], (D,), 0.3, 2.0, (), jnp.float32),
        "w_out": normal_values(part_splits[9], (D, 4), D ** -0.5, 0.1875),
        "b_out": normal_values(part_splits[10], (4,), 0.5, 3.0, (), jnp.float32),
    }


VISCOSITY = 0.05
DAMP_FACTOR = 1.0
DAMP_OUTPUT = 0.1

def point_weights(bin_row, count, bin_weight, slots):
    levels = jnp.arange(bin_weight.shape[0], dtype=jnp.int32)
    lookup = lax.optimization_barrier(jnp.sum(jnp.where(bin_row[None, :] == levels[:, None], bin_weight[:, None], jnp.float32(0.0)), 0))
    live = jnp.arange(slots, dtype=jnp.int32) < count
    return jnp.where(live, lookup, jnp.float32(0.0))

def taylor(points, w_in, b_in, w_mid, b_mid):
    width = w_mid.shape[0]
    pre = points[0][:, None] * w_in[0] + points[1][:, None] * w_in[1] + points[2][:, None] * w_in[2] + b_in
    act = jnp.tanh(pre)
    slope = 1.0 - act * act
    curve_in = lax.optimization_barrier(jnp.sum(w_in * w_in, 0))
    first = jnp.stack([act, slope * w_in[0], slope * w_in[1], slope * w_in[2], -2.0 * act * slope * curve_in]).astype(jnp.bfloat16)
    count = points.shape[1]
    mixed = jnp.dot(first.reshape(5 * count, width).astype(jnp.float32), w_mid.astype(jnp.float32), preferred_element_type=jnp.float32).reshape(5, count, width)
    act_two = jnp.tanh(mixed[0] + b_mid)
    slope_two = 1.0 - act_two * act_two
    grads = mixed[1:4]
    lap_two = slope_two * mixed[4] - 2.0 * act_two * slope_two * lax.optimization_barrier(jnp.sum(grads * grads, 0))
    return jnp.concatenate([act_two[None], slope_two[None] * grads, lap_two[None]], 0).astype(jnp.bfloat16)

def residual_loss(heads, points, pushes, weights):
    value = heads[0]
    slopes = heads[1:4]
    curve = heads[4]
    height = points[1]
    wall = 1.0 - height * height
    flat_zero = jnp.zeros_like(height)
    wall_slope = jnp.stack([flat_zero, -2.0 * height, flat_zero])
    vel = wall[:, None] * value[:, :3]
    vel_slope = wall_slope[:, :, None] * value[None, :, :3] + wall[None, :, None] * slopes[:, :, :3]
    vel_lap = -2.0 * value[:, :3] + 2.0 * lax.optimization_barrier(jnp.sum(wall_slope[:, :, None] * slopes[:, :, :3], 0)) + wall[:, None] * curve[:, :3]
    convect = lax.optimization_barrier(jnp.sum(vel.T[:, :, None] * vel_slope, 0))
    momentum = convect + slopes[:, :, 3].T - VISCOSITY * vel_lap - pushes.T
    divergence = vel_slope[0, :, 0] + vel_slope[1, :, 1] + vel_slope[2, :, 2]
    return 0.5 * jnp.sum(weights * (lax.optimization_barrier(jnp.sum(momentum * momentum, 1)) + divergence * divergence))

def block_terms(points, pushes, weights, w_in, b_in, w_mid, b_mid, w_out, b_out):
    jets = taylor(points, w_in, b_in, w_mid, b_mid)
    count = points.shape[1]
    width = w_mid.shape[0]
    flat = jets.reshape(5 * count, width)
    heads = jnp.dot(flat.astype(jnp.float32), w_out.astype(jnp.float32), preferred_element_type=jnp.float32).reshape(5, count, 4)
    heads = heads.at[0].add(b_out)
    cotangent = jax.grad(residual_loss)(heads, points, pushes, weights).reshape(5 * count, 4)
    grad_part = lax.dot_general(flat.astype(jnp.float32), cotangent.astype(jnp.bfloat16).astype(jnp.float32), (((0,), (0,)), ((), ())), preferred_element_type=jnp.float32)
    outer = lax.dot_general(cotangent.astype(jnp.float32), cotangent.astype(jnp.float32), (((0,), (0,)), ((), ())), precision=lax.Precision.HIGHEST, preferred_element_type=jnp.float32)
    scaled = (jets * weights[None, :, None]).astype(jnp.bfloat16).reshape(5 * count, width)
    return (flat, scaled, grad_part, outer, jnp.sum(weights))

def reference(coords, forcing, bins, counts, bin_weight, w_in, b_in, w_mid, b_mid, w_out, b_out):
    block_points = coords.reshape(3, N_DP, CAP).transpose(1, 0, 2)
    block_pushes = forcing.reshape(3, N_DP, CAP).transpose(1, 0, 2)
    block_bins = bins.reshape(N_DP, CAP)

    def accumulate(carry, item):
        gram, grad_sum, outer_sum, weight_sum = carry
        points, pushes, bin_row, count = item
        weights = point_weights(bin_row, count, bin_weight, CAP)
        flat, scaled, grad_part, outer, wsum = block_terms(points, pushes, weights, w_in, b_in, w_mid, b_mid, w_out, b_out)
        gram = gram + lax.dot_general(scaled.astype(jnp.float32), flat.astype(jnp.float32), (((0,), (0,)), ((), ())), preferred_element_type=jnp.float32)
        return ((gram, grad_sum + grad_part, outer_sum + outer, weight_sum + wsum), None)
    init = (jnp.zeros((D, D), jnp.float32), jnp.zeros((D, 4), jnp.float32), jnp.zeros((4, 4), jnp.float32), jnp.zeros((), jnp.float32))
    (gram, grad_sum, outer_sum, weight_sum), _ = lax.scan(accumulate, init, (block_points, block_pushes, block_bins, counts))
    ident = jnp.eye(D, dtype=jnp.float32)
    factor = gram / weight_sum + DAMP_FACTOR * ident
    bound = jnp.max(lax.optimization_barrier(jnp.sum(jnp.abs(factor), 1)))
    iterate = 2.0 / bound * ident - factor / (bound * bound)
    for step in range(ITERS - 1):
        product = jnp.dot(factor.astype(jnp.float32), iterate.astype(jnp.float32), precision=lax.Precision.HIGHEST, preferred_element_type=jnp.float32)
        iterate = 2.0 * iterate - jnp.dot(product.astype(jnp.float32), iterate.astype(jnp.float32), precision=lax.Precision.HIGHEST, preferred_element_type=jnp.float32)
    output_factor = 4.0 * outer_sum / jnp.trace(outer_sum) + DAMP_OUTPUT * jnp.eye(4, dtype=jnp.float32)
    merged = jnp.dot(iterate.astype(jnp.float32), (grad_sum / weight_sum).astype(jnp.float32), precision=lax.Precision.HIGHEST, preferred_element_type=jnp.float32)
    lower = jnp.linalg.cholesky(output_factor)
    update = jax.scipy.linalg.cho_solve((lower, True), merged.T).T
    return (update, iterate)
```

```python
import functools

import jax
import jax.numpy as jnp
from jax import lax
from jax.experimental import pallas as pl
from jax.experimental.pallas import tpu as pltpu
from jax.sharding import PartitionSpec as P

ITERS = 6
VISCOSITY = 0.05
DAMP_FACTOR = 1.0
DAMP_OUTPUT = 0.1

TILE = 256
MESH = pl.DeviceIdType.MESH
VMEM = pl.BlockSpec(memory_space=pltpu.VMEM)
BIG = 56 * 1024 * 1024
ROWS_DOT = (((1,), (1,)), ((), ()))
F32 = jnp.float32
BF16 = jnp.bfloat16


def packed_points(coords, forcing, bins, count, bin_weight, upper):
    slots = coords.shape[1]
    levels = jnp.arange(bin_weight.shape[0], dtype=jnp.int32)
    lookup = jnp.sum(jnp.where(bins[None, :] == levels[:, None], bin_weight[:, None], F32(0.0)), 0)
    every = jnp.concatenate([coords, forcing, lookup[None], jnp.zeros((1, slots), F32)], 0)
    live = jnp.arange(slots, dtype=jnp.int32) < count
    every = jnp.where(live[None, :], every, F32(0.0))
    return jnp.where(upper, every[:, ::-1], every)


def share_points(axis_size, own_ref, out_ref, held, send_sem, recv_sem):
    half = axis_size // 2
    me = lax.axis_index("dp")
    place = me // 2
    parity = me % 2
    barrier = pltpu.get_barrier_semaphore()
    for hop in range(1, half):
        other = (place + hop) % half
        pl.semaphore_signal(
            barrier, inc=1, device_id={"dp": other * 2 + parity}, device_id_type=MESH
        )
    pl.semaphore_wait(barrier, half - 1)
    copies = []
    for hop in range(1, half):
        other = (place + hop) % half
        copy = pltpu.make_async_remote_copy(
            src_ref=own_ref,
            dst_ref=held.at[place],
            send_sem=send_sem.at[hop],
            recv_sem=recv_sem.at[place],
            device_id={"dp": other * 2 + parity},
            device_id_type=MESH,
        )
        copy.start()
        copies.append(copy)
    held[place] = own_ref[...]
    for hop in range(1, half):
        source = (place + hop) % half
        pltpu.make_async_remote_copy(
            src_ref=own_ref,
            dst_ref=held.at[source],
            send_sem=send_sem.at[hop],
            recv_sem=recv_sem.at[source],
            device_id={"dp": source * 2 + parity},
            device_id_type=MESH,
        ).wait_recv()
    for pair in range(half // 2):
        out_ref[pair] = held[pair] + held[pair + half // 2]
    for copy in copies:
        copy.wait_send()


def point_loss(heads, height, pushes, weight):
    value, slopes, curve = heads[0], heads[1:4], heads[4]
    wall = 1.0 - height * height
    wall_slope = -2.0 * height
    vel = [wall * value[i] for i in range(3)]
    vel_slope = [[wall * slopes[k][i] for i in range(3)] for k in range(3)]
    for i in range(3):
        vel_slope[1][i] = wall_slope * value[i] + vel_slope[1][i]
    total = vel_slope[0][0] + vel_slope[1][1] + vel_slope[2][2]
    total = total * total
    for i in range(3):
        lap = -2.0 * value[i] + 2.0 * (wall_slope * slopes[1][i]) + wall * curve[i]
        convect = vel[0] * vel_slope[0][i] + vel[1] * vel_slope[1][i] + vel[2] * vel_slope[2][i]
        momentum = convect + slopes[i][3] - VISCOSITY * lap - pushes[i]
        total = total + momentum * momentum
    return 0.5 * (weight * total)


def point_terms(points_ref, cols_ref, mid_ref, out_ref, bias_ref, gram_ref, small_ref, first, jets, scaled):
    width = mid_ref.shape[0]
    slots = points_ref.shape[2]
    tiles = width // TILE
    step = pl.program_id(0)

    @pl.when(step == 0)
    def _():
        gram_ref[...] = jnp.zeros_like(gram_ref)
        small_ref[...] = jnp.zeros_like(small_ref)

    row = [points_ref[0, k : k + 1, :] for k in range(7)]
    weight = row[6]

    def column(part, k):
        return cols_ref[part * TILE : (part + 1) * TILE, k : k + 1]

    for part in range(tiles):
        rows = pl.ds(part * TILE, TILE)
        w = [column(part, k) for k in range(3)]
        pre = row[0] * w[0] + row[1] * w[1] + row[2] * w[2] + column(part, 3)
        act = jnp.tanh(pre)
        slope = 1.0 - act * act
        curve_in = w[0] * w[0] + w[1] * w[1] + w[2] * w[2]
        first[rows, 0:slots] = act.astype(BF16)
        for k in range(3):
            first[rows, (k + 1) * slots : (k + 2) * slots] = (slope * w[k]).astype(BF16)
        first[rows, 4 * slots : 5 * slots] = (-2.0 * act * slope * curve_in).astype(BF16)
    for part in range(tiles):
        rows = pl.ds(part * TILE, TILE)
        mixed = jnp.dot(mid_ref[rows, :], first[...], preferred_element_type=F32)
        mixed = [mixed[:, k * slots : (k + 1) * slots] for k in range(5)]
        act = jnp.tanh(mixed[0] + column(part, 4))
        slope = 1.0 - act * act
        squares = mixed[1] * mixed[1] + mixed[2] * mixed[2] + mixed[3] * mixed[3]
        jet = [act, slope * mixed[1], slope * mixed[2], slope * mixed[3]]
        jet.append(slope * mixed[4] - 2.0 * act * slope * squares)
        for k in range(5):
            half = jet[k].astype(BF16)
            jets[rows, k * slots : (k + 1) * slots] = half
            scaled[rows, k * slots : (k + 1) * slots] = (half.astype(F32) * weight).astype(BF16)
    block = 0
    for i in range(tiles):
        rows = pl.ds(i * TILE, TILE)
        part = lax.dot_general(
            scaled[rows, :], jets[i * TILE :, :], ROWS_DOT, preferred_element_type=F32
        )
        for j in range(tiles - i):
            gram_ref[block] += part[:, j * TILE : (j + 1) * TILE]
            block += 1
    heads = jnp.dot(out_ref[...], jets[...], preferred_element_type=F32)
    table = [[heads[i : i + 1, k * slots : (k + 1) * slots] for i in range(4)] for k in range(5)]
    table[0] = [table[0][i] + bias_ref[i : i + 1, 0:1] for i in range(4)]
    _, pull = jax.vjp(lambda t: point_loss(t, row[1], row[3:6], weight), table)
    (slant,) = pull(jnp.ones_like(weight))
    at = lax.broadcasted_iota(jnp.int32, (8, slots), 0)
    pieces = []
    for k in range(5):
        piece = jnp.zeros((8, slots), F32)
        for i in range(4):
            piece = jnp.where(at == i, slant[k][i], piece)
        if k == 0:
            piece = jnp.where(at == 4, weight, piece)
            piece = jnp.where(at == 5, F32(1.0), piece)
        pieces.append(piece)
    cot = jnp.concatenate(pieces, 1)
    small_ref[0:8, :] += lax.dot_general(
        cot.astype(BF16), jets[...], ROWS_DOT, preferred_element_type=F32
    )
    small_ref[8:16, 0:8] += lax.dot_general(
        cot, cot, ROWS_DOT, precision=lax.Precision.HIGHEST, preferred_element_type=F32
    )


def swap_sums(gram_ref, small_ref, gram_out, small_out, send_sem, recv_sem):
    other = lax.axis_index("dp")
    other = other + 1 - 2 * (other % 2)
    barrier = pltpu.get_barrier_semaphore()
    pl.semaphore_signal(barrier, inc=1, device_id={"dp": other}, device_id_type=MESH)
    pl.semaphore_wait(barrier, 1)
    copies = []
    for at, (source, target) in enumerate(((gram_ref, gram_out), (small_ref, small_out))):
        copy = pltpu.make_async_remote_copy(
            src_ref=source,
            dst_ref=target,
            send_sem=send_sem.at[at],
            recv_sem=recv_sem.at[at],
            device_id={"dp": other},
            device_id_type=MESH,
        )
        copy.start()
        copies.append(copy)
    for copy in copies:
        copy.wait()


def solve_rows(own_rows, gram_a, gram_b, small_a, small_b, inverse_ref, update_ref, full, high, low):
    width = full.shape[0]
    tiles = width // TILE
    first_row = pl.multiple_of(lax.axis_index("dp") * own_rows, own_rows)
    small = small_a[...] + small_b[...]
    weight_sum = small[12:13, 5:6]
    block = 0
    largest = jnp.zeros((1, 1), F32)
    for i in range(tiles):
        for j in range(i, tiles):
            piece = (gram_a[block] + gram_b[block]) / weight_sum
            block += 1
            if i == j:
                here = lax.broadcasted_iota(jnp.int32, (TILE, TILE), 0)
                there = lax.broadcasted_iota(jnp.int32, (TILE, TILE), 1)
                piece = piece + jnp.where(here == there, F32(DAMP_FACTOR), F32(0.0))
            full[i * TILE : (i + 1) * TILE, j * TILE : (j + 1) * TILE] = piece
            if i != j:
                full[j * TILE : (j + 1) * TILE, i * TILE : (i + 1) * TILE] = piece.T
    for i in range(tiles):
        sums = jnp.sum(jnp.abs(full[i * TILE : (i + 1) * TILE, :]), 1, keepdims=True)
        largest = jnp.maximum(largest, jnp.max(sums, 0, keepdims=True))
    shrink = 1.0 / largest

    def put(at, rows, value):
        full[rows, :] = value
        upper = value.astype(BF16)
        high[at, rows, :] = upper
        low[rows, :] = (value - upper.astype(F32)).astype(BF16)

    for i in range(tiles):
        rows = pl.ds(i * TILE, TILE)
        put(0, rows, full[rows, :] * shrink)
    mine = full[pl.ds(first_row, own_rows), :]
    at_row = lax.broadcasted_iota(jnp.int32, mine.shape, 0) + first_row
    at_col = lax.broadcasted_iota(jnp.int32, mine.shape, 1)
    iterate = jnp.where(at_row == at_col, F32(2.0), F32(0.0)) - mine

    def times(value, at):
        upper = value.astype(BF16)
        lower = (value - upper.astype(F32)).astype(BF16)
        both = jnp.dot(jnp.concatenate([upper, lower], 0), high[at], preferred_element_type=F32)
        rest = jnp.dot(upper, low[...], preferred_element_type=F32)
        return both[:own_rows] + (both[own_rows:] + rest)

    at = 0
    for _ in range(ITERS - 2):
        for i in range(tiles):
            rows = pl.ds(i * TILE, TILE)
            square = jnp.dot(high[at, rows, :], high[at], preferred_element_type=F32)
            put(1 - at, rows, 2.0 * full[rows, :] - square)
        at = 1 - at
        iterate = 2.0 * iterate - times(iterate, at)
    turned = iterate - times(iterate, at)
    turned = turned - times(turned, at)
    iterate = (iterate + turned) * shrink
    inverse_ref[...] = iterate
    merged = lax.dot_general(
        small[0:8, :] / weight_sum,
        iterate,
        ROWS_DOT,
        precision=lax.Precision.HIGHEST,
        preferred_element_type=F32,
    )
    outer = [[small[8 + i : 9 + i, j : j + 1] for j in range(4)] for i in range(4)]
    trace = outer[0][0] + outer[1][1] + outer[2][2] + outer[3][3]
    lower = [[None] * 4 for _ in range(4)]
    for i in range(4):
        for j in range(i + 1):
            entry = 4.0 * outer[i][j] / trace
            if i == j:
                entry = entry + DAMP_OUTPUT
            for k in range(j):
                entry = entry - lower[i][k] * lower[j][k]
            lower[i][j] = jnp.sqrt(entry) if i == j else entry / lower[j][j]
    solved = [merged[i : i + 1, :] for i in range(4)]
    for i in range(4):
        for k in range(i):
            solved[i] = solved[i] - lower[i][k] * solved[k]
        solved[i] = solved[i] / lower[i][i]
    for i in reversed(range(4)):
        for k in range(i + 1, 4):
            solved[i] = solved[i] - lower[k][i] * solved[k]
        solved[i] = solved[i] / lower[i][i]
    at = lax.broadcasted_iota(jnp.int32, (8, own_rows), 0)
    update = jnp.zeros((8, own_rows), F32)
    for i in range(4):
        update = jnp.where(at == i, solved[i], update)
    update_ref[...] = update


def on_device(coords, forcing, bins, counts, bin_weight, w_in, b_in, w_mid, b_mid, w_out, b_out):
    slots = coords.shape[1]
    width = w_mid.shape[0]
    size = lax.axis_size("dp")
    half = size // 2
    pairs = half // 2
    tiles = width // TILE
    blocks = tiles * (tiles + 1) // 2
    own_rows = width // size
    upper = lax.axis_index("dp") >= half
    own = packed_points(coords, forcing, bins, counts[0], bin_weight, upper)
    points = pl.pallas_call(
        functools.partial(share_points, size),
        out_shape=jax.ShapeDtypeStruct((pairs, 8, slots), F32),
        in_specs=[VMEM],
        out_specs=VMEM,
        scratch_shapes=[
            pltpu.VMEM((half, 8, slots), F32),
            pltpu.SemaphoreType.DMA((half,)),
            pltpu.SemaphoreType.DMA((half,)),
        ],
        compiler_params=pltpu.CompilerParams(collective_id=0, has_side_effects=True),
        name="share_points",
    )(own)
    cols = jnp.concatenate([w_in, b_in[None], b_mid[None], jnp.zeros((3, width), F32)], 0).T
    out_rows = jnp.concatenate([w_out.T, jnp.zeros((12, width), BF16)], 0)
    bias = jnp.concatenate([b_out, jnp.zeros((4,), F32)])[:, None]
    fixed = lambda *shape: pl.BlockSpec(shape, lambda i: (0,) * len(shape))
    gram, small = pl.pallas_call(
        point_terms,
        grid=(pairs,),
        out_shape=(
            jax.ShapeDtypeStruct((blocks, TILE, TILE), F32),
            jax.ShapeDtypeStruct((16, width), F32),
        ),
        in_specs=[
            pl.BlockSpec((1, 8, slots), lambda i: (i, 0, 0)),
            fixed(width, 8),
            fixed(width, width),
            fixed(16, width),
            fixed(8, 1),
        ],
        out_specs=(fixed(blocks, TILE, TILE), fixed(16, width)),
        scratch_shapes=[pltpu.VMEM((width, 5 * slots), BF16) for _ in range(3)],
        compiler_params=pltpu.CompilerParams(vmem_limit_bytes=BIG),
        name="point_terms",
    )(points, cols, w_mid.T, out_rows, bias)
    gram_other, small_other = pl.pallas_call(
        swap_sums,
        out_shape=(
            jax.ShapeDtypeStruct(gram.shape, F32),
            jax.ShapeDtypeStruct(small.shape, F32),
        ),
        in_specs=[VMEM, VMEM],
        out_specs=(VMEM, VMEM),
        scratch_shapes=[pltpu.SemaphoreType.DMA((2,)), pltpu.SemaphoreType.DMA((2,))],
        compiler_params=pltpu.CompilerParams(
            collective_id=1, has_side_effects=True, vmem_limit_bytes=BIG
        ),
        name="swap_sums",
    )(gram, small)
    inverse, update = pl.pallas_call(
        functools.partial(solve_rows, own_rows),
        out_shape=(
            jax.ShapeDtypeStruct((own_rows, width), F32),
            jax.ShapeDtypeStruct((8, own_rows), F32),
        ),
        in_specs=[VMEM] * 4,
        out_specs=(VMEM, VMEM),
        scratch_shapes=[
            pltpu.VMEM((width, width), F32),
            pltpu.VMEM((2, width, width), BF16),
            pltpu.VMEM((width, width), BF16),
        ],
        compiler_params=pltpu.CompilerParams(vmem_limit_bytes=BIG),
        name="solve_rows",
    )(gram, gram_other, small, small_other)
    return (update[:4].T, inverse)


def solution(mesh):
    placed = (
        P(None, ("groups", "dp")),
        P(None, ("groups", "dp")),
        P(("groups", "dp")),
        P(("groups", "dp")),
        P("groups"),
        P("groups", None),
        P("groups"),
        P("groups", None),
        P("groups"),
        P("groups", None),
        P("groups"),
    )
    return jax.shard_map(
        on_device,
        mesh=mesh,
        in_specs=placed,
        out_specs=(P(("groups", "dp"), None), P(("groups", "dp"), None)),
        check_vma=False,
    )
```

```python
import functools

import jax
import jax.numpy as jnp
from jax import lax
from jax.experimental import pallas as pl
from jax.experimental.pallas import tpu as pltpu
from jax.sharding import PartitionSpec as P

ITERS = 6
VISCOSITY = 0.05
DAMP_FACTOR = 1.0
DAMP_OUTPUT = 0.1

TILE = 256
MESH = pl.DeviceIdType.MESH
VMEM = pl.BlockSpec(memory_space=pltpu.VMEM)
BIG = 56 * 1024 * 1024
ROWS_DOT = (((1,), (1,)), ((), ()))
F32 = jnp.float32
BF16 = jnp.bfloat16


def share_points(
    axis_size, coords_ref, forcing_ref, bins_ref, count_ref, level_ref, w_in_ref, b_in_ref, b_mid_ref,
    mid_ref, out_ref, cols_ref, mid_out, own, held, plain, turned, send_sem, recv_sem, local_sem,
):
    half = axis_size // 2
    me = lax.axis_index("dp")
    place = me // 2
    parity = me % 2
    slots = coords_ref.shape[1]
    width = mid_ref.shape[0]
    tiles = width // TILE
    fetch = pltpu.make_async_copy(mid_ref, plain, local_sem.at[0])
    fetch.start()
    barrier = pltpu.get_barrier_semaphore()
    for hop in range(1, half):
        other = (place + hop) % half
        pl.semaphore_signal(
            barrier, inc=1, device_id={"dp": other * 2 + parity}, device_id_type=MESH
        )
    bins = bins_ref[...]
    weight = jnp.zeros((1, slots), F32)
    for level in range(level_ref.shape[1]):
        weight = jnp.where(bins == level, level_ref[0:1, level : level + 1], weight)
    at = lax.broadcasted_iota(jnp.int32, (8, slots), 0)
    every = jnp.zeros((8, slots), F32)
    for k in range(3):
        every = jnp.where(at == k, coords_ref[k : k + 1, :], every)
        every = jnp.where(at == 3 + k, forcing_ref[k : k + 1, :], every)
    every = jnp.where(at == 6, weight, every)
    slot = lax.broadcasted_iota(jnp.int32, (8, slots), 1)
    every = jnp.where(slot < count_ref[0:1, 0:1], every, F32(0.0))
    source = lax.broadcasted_iota(jnp.int32, (slots, slots), 0)
    target = lax.broadcasted_iota(jnp.int32, (slots, slots), 1)
    target = jnp.where(me >= half, slots - 1 - target, target)
    move = jnp.where(source == target, F32(1.0), F32(0.0))
    own[...] = jnp.dot(
        every, move, precision=lax.Precision.HIGHEST, preferred_element_type=F32
    )
    pl.semaphore_wait(barrier, half - 1)
    copies = []
    for hop in range(1, half):
        other = (place + hop) % half
        copy = pltpu.make_async_remote_copy(
            src_ref=own,
            dst_ref=held.at[place],
            send_sem=send_sem.at[hop],
            recv_sem=recv_sem.at[place],
            device_id={"dp": other * 2 + parity},
            device_id_type=MESH,
        )
        copy.start()
        copies.append(copy)
    held[place] = own[...]
    table = jnp.zeros((8, width), F32)
    at = lax.broadcasted_iota(jnp.int32, (8, width), 0)
    for k in range(3):
        table = jnp.where(at == k, w_in_ref[k : k + 1, :], table)
    table = jnp.where(at == 3, b_in_ref[...], table)
    table = jnp.where(at == 4, b_mid_ref[...], table)
    cols_ref[...] = table.T
    fetch.wait()
    for i in range(tiles):
        for j in range(tiles):
            turned[j * TILE : (j + 1) * TILE, i * TILE : (i + 1) * TILE] = plain[
                i * TILE : (i + 1) * TILE, j * TILE : (j + 1) * TILE
            ].T
    give = pltpu.make_async_copy(turned, mid_out, local_sem.at[1])
    give.start()
    for hop in range(1, half):
        other = (place + hop) % half
        pltpu.make_async_remote_copy(
            src_ref=own,
            dst_ref=held.at[other],
            send_sem=send_sem.at[hop],
            recv_sem=recv_sem.at[other],
            device_id={"dp": other * 2 + parity},
            device_id_type=MESH,
        ).wait_recv()
    for pair in range(half // 2):
        out_ref[pair] = held[pair] + held[pair + half // 2]
    for copy in copies:
        copy.wait_send()
    give.wait()


def point_loss(heads, height, pushes, weight):
    value, slopes, curve = heads[0], heads[1:4], heads[4]
    wall = 1.0 - height * height
    wall_slope = -2.0 * height
    vel = [wall * value[i] for i in range(3)]
    vel_slope = [[wall * slopes[k][i] for i in range(3)] for k in range(3)]
    for i in range(3):
        vel_slope[1][i] = wall_slope * value[i] + vel_slope[1][i]
    total = vel_slope[0][0] + vel_slope[1][1] + vel_slope[2][2]
    total = total * total
    for i in range(3):
        lap = -2.0 * value[i] + 2.0 * (wall_slope * slopes[1][i]) + wall * curve[i]
        convect = vel[0] * vel_slope[0][i] + vel[1] * vel_slope[1][i] + vel[2] * vel_slope[2][i]
        momentum = convect + slopes[i][3] - VISCOSITY * lap - pushes[i]
        total = total + momentum * momentum
    return 0.5 * (weight * total)


def point_terms(points_ref, cols_ref, mid_ref, out_ref, bias_ref, gram_ref, small_ref, first, jets, scaled):
    width = mid_ref.shape[0]
    pairs, _, slots = points_ref.shape
    tiles = width // TILE
    step = pl.program_id(0)

    def column(part, k):
        return cols_ref[part * TILE : (part + 1) * TILE, k : k + 1]

    def first_jet(part):
        row = [points_ref[step, k : k + 1, :] for k in range(3)]
        rows = slice(part * TILE, (part + 1) * TILE)
        w = [column(part, k) for k in range(3)]
        pre = row[0] * w[0] + row[1] * w[1] + row[2] * w[2] + column(part, 3)
        act = jnp.tanh(pre)
        slope = 1.0 - act * act
        curve_in = -2.0 * (w[0] * w[0] + w[1] * w[1] + w[2] * w[2])
        first[rows, 0:slots] = act.astype(BF16)
        for k in range(3):
            first[rows, (k + 1) * slots : (k + 2) * slots] = (slope * w[k]).astype(BF16)
        first[rows, 4 * slots : 5 * slots] = (act * slope * curve_in).astype(BF16)

    def hidden_mixed(part):
        rows = slice(part * TILE, (part + 1) * TILE)
        return jnp.dot(mid_ref[rows, :], first[...], preferred_element_type=F32)

    def hidden_jet(part, mixed):
        weight = points_ref[step, 6:7, :]
        mixed = [mixed[:, k * slots : (k + 1) * slots] for k in range(5)]
        act = jnp.tanh(mixed[0] + column(part, 4))
        slope = 1.0 - act * act
        squares = mixed[1] * mixed[1] + mixed[2] * mixed[2] + mixed[3] * mixed[3]
        jet = [act, slope * mixed[1], slope * mixed[2], slope * mixed[3]]
        jet.append(slope * (mixed[4] - 2.0 * act * squares))
        for k in range(5):
            half = jet[k].astype(BF16)
            places = slice(k * slots, (k + 1) * slots)
            jets[part * TILE : (part + 1) * TILE, places] = half
            scaled[16 + part * TILE : 16 + (part + 1) * TILE, places] = (
                half.astype(F32) * weight
            ).astype(BF16)

    def gram_rows(i):
        start = 0 if i == 0 else 16 + i * TILE
        part = lax.dot_general(
            scaled[start : 16 + (i + 1) * TILE, :],
            jets[i * TILE :, :],
            ROWS_DOT,
            preferred_element_type=F32,
        )
        if i == 0:
            small_ref[0:8, :] += part[0:8, :]
            part = part[16:, :]
        block = i * tiles - i * (i - 1) // 2
        for j in range(tiles - i):
            gram_ref[block + j] += part[:, j * TILE : (j + 1) * TILE]

    def slants():
        row = [points_ref[step - 1, k : k + 1, :] for k in range(7)]
        weight = row[6]
        heads = jnp.dot(out_ref[...], jets[...], preferred_element_type=F32)
        table = [[heads[i : i + 1, k * slots : (k + 1) * slots] for i in range(4)] for k in range(5)]
        table[0] = [table[0][i] + bias_ref[0:1, i : i + 1] for i in range(4)]
        _, pull = jax.vjp(lambda t: point_loss(t, row[1], row[3:6], weight), table)
        (slant,) = pull(jnp.ones_like(weight))
        at = lax.broadcasted_iota(jnp.int32, (16, slots), 0)
        pieces = []
        for k in range(5):
            piece = jnp.zeros((16, slots), F32)
            for i in range(4):
                piece = jnp.where(at == i, slant[k][i], piece)
            if k == 0:
                piece = jnp.where(at == 4, weight, piece)
                piece = jnp.where(at == 5, F32(1.0), piece)
            pieces.append(piece)
        cot = jnp.concatenate(pieces, 1)
        scaled[0:16, :] = cot.astype(BF16)
        small_ref[8:16, 0:8] += lax.dot_general(
            cot[0:8],
            cot[0:8],
            ROWS_DOT,
            precision=lax.Precision.HIGHEST,
            preferred_element_type=F32,
        )

    @pl.when(step == 0)
    def _():
        gram_ref[...] = jnp.zeros_like(gram_ref)
        small_ref[...] = jnp.zeros_like(small_ref)
        for part in range(tiles):
            first_jet(part)

    @pl.when((step > 0) & (step < pairs))
    def _():
        slants()
        for part in range(tiles):
            gram_rows(tiles - 1 - part)
            first_jet(part)

    @pl.when(step == pairs)
    def _():
        slants()
        for part in range(tiles):
            gram_rows(tiles - 1 - part)

    @pl.when(step < pairs)
    def _():
        mixed = hidden_mixed(0)
        for part in range(tiles):
            later = hidden_mixed(part + 1) if part + 1 < tiles else None
            hidden_jet(part, mixed)
            mixed = later


def solve_rows(
    own_rows, gram_ref, small_ref, inverse_ref, update_ref,
    gram_a, gram_b, small_b, full, high, send_sem, recv_sem, local_sem,
):
    width = full.shape[0]
    tiles = width // TILE
    blocks = gram_a.shape[0]
    me = lax.axis_index("dp")
    first_row = pl.multiple_of(me * own_rows, own_rows)
    other = me + 1 - 2 * (me % 2)
    fetch = pltpu.make_async_copy(gram_ref, gram_a, local_sem.at[0])
    fetch.start()
    barrier = pltpu.get_barrier_semaphore()
    pl.semaphore_signal(barrier, inc=1, device_id={"dp": other}, device_id_type=MESH)
    pl.semaphore_wait(barrier, 1)
    copies = []
    for at in range(blocks + 1):
        copy = pltpu.make_async_remote_copy(
            src_ref=gram_ref.at[at] if at < blocks else small_ref,
            dst_ref=gram_b.at[at] if at < blocks else small_b,
            send_sem=send_sem.at[at],
            recv_sem=recv_sem.at[at],
            device_id={"dp": other},
            device_id_type=MESH,
        )
        copies.append(copy)
    for copy in copies[-1:] + copies[:-1]:
        copy.start()
    copies[-1].wait_recv()
    small = small_ref[...] + small_b[...]
    weight_sum = small[12:13, 5:6]
    share = 1.0 / weight_sum
    fetch.wait()
    sums = [jnp.zeros((1, TILE), F32) for _ in range(tiles)]
    here = lax.broadcasted_iota(jnp.int32, (TILE, TILE), 0)
    there = lax.broadcasted_iota(jnp.int32, (TILE, TILE), 1)
    damp = jnp.where(here == there, F32(DAMP_FACTOR), F32(0.0))
    block = 0
    for i in range(tiles):
        for j in range(i, tiles):
            copies[block].wait_recv()
            piece = (gram_a[block] + gram_b[block]) * share
            block += 1
            if i == j:
                piece = piece + damp
            turned = piece.T
            rows, cols = slice(i * TILE, (i + 1) * TILE), slice(j * TILE, (j + 1) * TILE)
            full[rows, cols] = piece
            high[0, rows, cols] = piece.astype(BF16)
            sums[i] = sums[i] + jnp.sum(jnp.abs(turned), 0, keepdims=True)
            if i != j:
                full[cols, rows] = turned
                high[0, cols, rows] = turned.astype(BF16)
                sums[j] = sums[j] + jnp.sum(jnp.abs(piece), 0, keepdims=True)
    for copy in copies:
        copy.wait_send()
    largest = functools.reduce(jnp.maximum, sums)
    shrink = 1.0 / jnp.max(largest, 1, keepdims=True)
    mine = full[pl.ds(first_row, own_rows), :]
    at_row = lax.broadcasted_iota(jnp.int32, mine.shape, 0) + first_row
    at_col = lax.broadcasted_iota(jnp.int32, mine.shape, 1)
    iterate = jnp.where(at_row == at_col, F32(2.0), F32(0.0)) - mine * shrink

    def split(value):
        upper = value.astype(BF16)
        return upper, (value - upper.astype(F32)).astype(BF16)

    def times(value, at):
        both = jnp.concatenate(split(value), 0)
        both = jnp.dot(both, high[at, 0:width, :], preferred_element_type=F32)
        return both[:own_rows] + both[own_rows:]

    at = 0
    for turn in range(ITERS - 2):
        if turn > 0:
            upper, lower = split(iterate)
            high[at, width : width + own_rows, :] = upper
            high[at, width + own_rows : width + 2 * own_rows, :] = lower
        reach = width + 2 * own_rows if turn > 0 else width
        products = []
        for j in range(tiles):
            cols = slice(j * TILE, (j + 1) * TILE)
            square = jnp.dot(
                high[at, 0:reach, :], high[at, 0:width, cols], preferred_element_type=F32
            )
            if turn == 0:
                later = shrink * (2.0 * full[:, cols] - shrink * square)
            else:
                later = 2.0 * full[:, cols] - square[0:width]
                products.append(
                    square[width : width + own_rows] + square[width + own_rows :]
                )
            full[:, cols] = later
            high[1 - at, 0:width, cols] = later.astype(BF16)
        if turn > 0:
            iterate = 2.0 * iterate - jnp.concatenate(products, 1)
        at = 1 - at
    iterate = 2.0 * iterate - times(iterate, at)
    turned = iterate - times(iterate, at)
    turned = turned - times(turned, at)
    iterate = (iterate + turned) * shrink
    inverse_ref[...] = iterate
    merged = lax.dot_general(
        small[0:8, :] / weight_sum,
        iterate,
        ROWS_DOT,
        precision=lax.Precision.HIGHEST,
        preferred_element_type=F32,
    )
    outer = [[small[8 + i : 9 + i, j : j + 1] for j in range(4)] for i in range(4)]
    trace = outer[0][0] + outer[1][1] + outer[2][2] + outer[3][3]
    lower = [[None] * 4 for _ in range(4)]
    for i in range(4):
        for j in range(i + 1):
            entry = 4.0 * outer[i][j] / trace
            if i == j:
                entry = entry + DAMP_OUTPUT
            for k in range(j):
                entry = entry - lower[i][k] * lower[j][k]
            lower[i][j] = jnp.sqrt(entry) if i == j else entry / lower[j][j]
    solved = [merged[i : i + 1, :] for i in range(4)]
    for i in range(4):
        for k in range(i):
            solved[i] = solved[i] - lower[i][k] * solved[k]
        solved[i] = solved[i] / lower[i][i]
    for i in reversed(range(4)):
        for k in range(i + 1, 4):
            solved[i] = solved[i] - lower[k][i] * solved[k]
        solved[i] = solved[i] / lower[i][i]
    at = lax.broadcasted_iota(jnp.int32, (4, own_rows), 0)
    update = jnp.zeros((4, own_rows), F32)
    for i in range(4):
        update = jnp.where(at == i, solved[i], update)
    update_ref[...] = update


def on_device(coords, forcing, bins, counts, bin_weight, w_in, b_in, w_mid, b_mid, w_out, b_out):
    slots = coords.shape[1]
    width = w_mid.shape[0]
    size = lax.axis_size("dp")
    half = size // 2
    pairs = half // 2
    tiles = width // TILE
    blocks = tiles * (tiles + 1) // 2
    own_rows = width // size
    points, cols, mid = pl.pallas_call(
        functools.partial(share_points, size),
        out_shape=(
            jax.ShapeDtypeStruct((pairs, 8, slots), F32),
            jax.ShapeDtypeStruct((width, 8), F32),
            jax.ShapeDtypeStruct((width, width), BF16),
        ),
        in_specs=[VMEM] * 8 + [pl.BlockSpec(memory_space=pl.ANY)],
        out_specs=(VMEM, VMEM, pl.BlockSpec(memory_space=pl.ANY)),
        scratch_shapes=[
            pltpu.VMEM((8, slots), F32),
            pltpu.VMEM((half, 8, slots), F32),
            pltpu.VMEM((width, width), BF16),
            pltpu.VMEM((width, width), BF16),
            pltpu.SemaphoreType.DMA((half,)),
            pltpu.SemaphoreType.DMA((half,)),
            pltpu.SemaphoreType.DMA((2,)),
        ],
        compiler_params=pltpu.CompilerParams(
            collective_id=0, has_side_effects=True, vmem_limit_bytes=BIG
        ),
        name="share_points",
    )(
        coords, forcing, bins[None], counts[None], bin_weight[None], w_in, b_in[None], b_mid[None],
        w_mid,
    )
    fixed = lambda *shape: pl.BlockSpec(shape, lambda i: (0,) * len(shape))
    gram, small = pl.pallas_call(
        point_terms,
        grid=(pairs + 1,),
        out_shape=(
            jax.ShapeDtypeStruct((blocks, TILE, TILE), F32),
            jax.ShapeDtypeStruct((16, width), F32),
        ),
        in_specs=[
            fixed(pairs, 8, slots),
            fixed(width, 8),
            fixed(width, width),
            fixed(4, width),
            fixed(1, 4),
        ],
        out_specs=(fixed(blocks, TILE, TILE), fixed(16, width)),
        scratch_shapes=[
            pltpu.VMEM((width, 5 * slots), BF16),
            pltpu.VMEM((width, 5 * slots), BF16),
            pltpu.VMEM((width + 16, 5 * slots), BF16),
        ],
        compiler_params=pltpu.CompilerParams(vmem_limit_bytes=BIG),
        name="point_terms",
    )(points, cols, mid, w_out.T, b_out[None])
    inverse, update = pl.pallas_call(
        functools.partial(solve_rows, own_rows),
        out_shape=(
            jax.ShapeDtypeStruct((own_rows, width), F32),
            jax.ShapeDtypeStruct((4, own_rows), F32),
        ),
        in_specs=[pl.BlockSpec(memory_space=pl.ANY), VMEM],
        out_specs=(VMEM, VMEM),
        scratch_shapes=[
            pltpu.VMEM((blocks, TILE, TILE), F32),
            pltpu.VMEM((blocks, TILE, TILE), F32),
            pltpu.VMEM((16, width), F32),
            pltpu.VMEM((width, width), F32),
            pltpu.VMEM((2, width + 2 * own_rows, width), BF16),
            pltpu.SemaphoreType.DMA((blocks + 1,)),
            pltpu.SemaphoreType.DMA((blocks + 1,)),
            pltpu.SemaphoreType.DMA((1,)),
        ],
        compiler_params=pltpu.CompilerParams(
            collective_id=1, has_side_effects=True, vmem_limit_bytes=BIG
        ),
        name="solve_rows",
    )(gram, small)
    return (update.T, inverse)


def solution(mesh):
    placed = (
        P(None, ("groups", "dp")),
        P(None, ("groups", "dp")),
        P(("groups", "dp")),
        P(("groups", "dp")),
        P("groups"),
        P("groups", None),
        P("groups"),
        P("groups", None),
        P("groups"),
        P("groups", None),
        P("groups"),
    )
    return jax.shard_map(
        on_device,
        mesh=mesh,
        in_specs=placed,
        out_specs=(P(("groups", "dp"), None), P(("groups", "dp"), None)),
        check_vma=False,
    )
```

```python
import functools

import jax
import jax.numpy as jnp
from jax import lax
from jax.experimental import pallas as pl
from jax.experimental.pallas import tpu as pltpu
from jax.sharding import PartitionSpec as P

ITERS = 6
VISCOSITY = 0.05
DAMP_FACTOR = 1.0
DAMP_OUTPUT = 0.1

TILE = 256
MESH = pl.DeviceIdType.MESH
VMEM = pl.BlockSpec(memory_space=pltpu.VMEM)
BIG = 56 * 1024 * 1024
ROWS_DOT = (((1,), (1,)), ((), ()))
F32 = jnp.float32
BF16 = jnp.bfloat16


def share_points(
    axis_size, coords_ref, forcing_ref, bins_ref, count_ref, level_ref, w_in_ref, b_in_ref, b_mid_ref,
    mid_ref, out_ref, cols_ref, mid_out, own, held, plain, turned, send_sem, recv_sem, local_sem,
):
    half = axis_size // 2
    me = lax.axis_index("dp")
    place = me // 2
    parity = me % 2
    slots = coords_ref.shape[1]
    width = mid_ref.shape[0]
    tiles = width // TILE
    fetch = pltpu.make_async_copy(mid_ref, plain, local_sem.at[0])
    fetch.start()
    barrier = pltpu.get_barrier_semaphore()
    for hop in range(1, half):
        other = (place + hop) % half
        pl.semaphore_signal(
            barrier, inc=1, device_id={"dp": other * 2 + parity}, device_id_type=MESH
        )
    bins = bins_ref[...]
    weight = jnp.zeros((1, slots), F32)
    for level in range(level_ref.shape[1]):
        weight = jnp.where(bins == level, level_ref[0:1, level : level + 1], weight)
    at = lax.broadcasted_iota(jnp.int32, (8, slots), 0)
    every = jnp.zeros((8, slots), F32)
    for k in range(3):
        every = jnp.where(at == k, coords_ref[k : k + 1, :], every)
        every = jnp.where(at == 3 + k, forcing_ref[k : k + 1, :], every)
    every = jnp.where(at == 6, weight, every)
    slot = lax.broadcasted_iota(jnp.int32, (8, slots), 1)
    every = jnp.where(slot < count_ref[0:1, 0:1], every, F32(0.0))
    source = lax.broadcasted_iota(jnp.int32, (slots, slots), 0)
    target = lax.broadcasted_iota(jnp.int32, (slots, slots), 1)
    target = jnp.where(me >= half, slots - 1 - target, target)
    move = jnp.where(source == target, F32(1.0), F32(0.0))
    own[...] = jnp.dot(
        every, move, precision=lax.Precision.HIGHEST, preferred_element_type=F32
    )
    pl.semaphore_wait(barrier, half - 1)
    copies = []
    for hop in range(1, half):
        other = (place + hop) % half
        copy = pltpu.make_async_remote_copy(
            src_ref=own,
            dst_ref=held.at[place],
            send_sem=send_sem.at[hop],
            recv_sem=recv_sem.at[place],
            device_id={"dp": other * 2 + parity},
            device_id_type=MESH,
        )
        copy.start()
        copies.append(copy)
    held[place] = own[...]
    table = jnp.zeros((8, width), F32)
    at = lax.broadcasted_iota(jnp.int32, (8, width), 0)
    for k in range(3):
        table = jnp.where(at == k, w_in_ref[k : k + 1, :], table)
    table = jnp.where(at == 3, b_in_ref[...], table)
    table = jnp.where(at == 4, b_mid_ref[...], table)
    cols_ref[...] = table.T
    fetch.wait()
    for i in range(tiles):
        for j in range(tiles):
            turned[j * TILE : (j + 1) * TILE, i * TILE : (i + 1) * TILE] = plain[
                i * TILE : (i + 1) * TILE, j * TILE : (j + 1) * TILE
            ].T
    give = pltpu.make_async_copy(turned, mid_out, local_sem.at[1])
    give.start()
    for hop in range(1, half):
        other = (place + hop) % half
        pltpu.make_async_remote_copy(
            src_ref=own,
            dst_ref=held.at[other],
            send_sem=send_sem.at[hop],
            recv_sem=recv_sem.at[other],
            device_id={"dp": other * 2 + parity},
            device_id_type=MESH,
        ).wait_recv()
    for pair in range(half // 2):
        out_ref[pair] = held[pair] + held[pair + half // 2]
    for copy in copies:
        copy.wait_send()
    give.wait()


def point_loss(heads, height, pushes, weight):
    value, slopes, curve = heads[0], heads[1:4], heads[4]
    wall = 1.0 - height * height
    wall_slope = -2.0 * height
    vel = [wall * value[i] for i in range(3)]
    vel_slope = [[wall * slopes[k][i] for i in range(3)] for k in range(3)]
    for i in range(3):
        vel_slope[1][i] = wall_slope * value[i] + vel_slope[1][i]
    total = vel_slope[0][0] + vel_slope[1][1] + vel_slope[2][2]
    total = total * total
    for i in range(3):
        lap = -2.0 * value[i] + 2.0 * (wall_slope * slopes[1][i]) + wall * curve[i]
        convect = vel[0] * vel_slope[0][i] + vel[1] * vel_slope[1][i] + vel[2] * vel_slope[2][i]
        momentum = convect + slopes[i][3] - VISCOSITY * lap - pushes[i]
        total = total + momentum * momentum
    return 0.5 * (weight * total)


def point_terms(points_ref, cols_ref, mid_ref, out_ref, bias_ref, gram_ref, small_ref, first, jets, scaled, gram_b, small_b, send_sem, recv_sem):
    width = mid_ref.shape[0]
    pairs, _, slots = points_ref.shape
    tiles = width // TILE
    step = pl.program_id(0)
    me = lax.axis_index("dp")
    other = me + 1 - 2 * (me % 2)
    barrier = pltpu.get_barrier_semaphore()

    def column(part, k):
        return cols_ref[part * TILE : (part + 1) * TILE, k : k + 1]

    def first_jet(part):
        row = [points_ref[step, k : k + 1, :] for k in range(3)]
        rows = slice(part * TILE, (part + 1) * TILE)
        w = [column(part, k) for k in range(3)]
        pre = row[0] * w[0] + row[1] * w[1] + row[2] * w[2] + column(part, 3)
        act = jnp.tanh(pre)
        slope = 1.0 - act * act
        curve_in = -2.0 * (w[0] * w[0] + w[1] * w[1] + w[2] * w[2])
        first[rows, 0:slots] = act.astype(BF16)
        for k in range(3):
            first[rows, (k + 1) * slots : (k + 2) * slots] = (slope * w[k]).astype(BF16)
        first[rows, 4 * slots : 5 * slots] = (act * slope * curve_in).astype(BF16)

    def hidden_mixed(part, k):
        rows = slice(part * TILE, (part + 1) * TILE)
        return jnp.dot(
            mid_ref[rows, :], first[:, k * slots : (k + 1) * slots], preferred_element_type=F32
        )

    def keep_jet(part, k, jet):
        weight = points_ref[step, 6:7, :]
        places = slice(k * slots, (k + 1) * slots)
        jets[part * TILE : (part + 1) * TILE, places] = jet.astype(BF16)
        scaled[16 + part * TILE : 16 + (part + 1) * TILE, places] = (jet * weight).astype(BF16)

    def hidden_jets():
        mixed = [hidden_mixed(0, k) for k in range(5)]
        for part in range(tiles):
            later = []
            for k in range(5):
                if part + 1 < tiles:
                    later.append(hidden_mixed(part + 1, k))
                if k == 0:
                    act = jnp.tanh(mixed[0] + column(part, 4))
                    slope = 1.0 - act * act
                    jet = act
                elif k < 4:
                    square = mixed[k] * mixed[k]
                    squares = square if k == 1 else squares + square
                    jet = slope * mixed[k]
                else:
                    jet = slope * (mixed[4] - 2.0 * act * squares)
                keep_jet(part, k, jet)
            mixed = later

    def gram_rows(i):
        start = 0 if i == 0 else 16 + i * TILE
        part = lax.dot_general(
            scaled[start : 16 + (i + 1) * TILE, :],
            jets[i * TILE :, :],
            ROWS_DOT,
            preferred_element_type=F32,
        )
        if i == 0:
            small_ref[0:8, :] += part[0:8, :]
            part = part[16:, :]
        block = i * tiles - i * (i - 1) // 2
        for j in range(tiles - i):
            gram_ref[block + j] += part[:, j * TILE : (j + 1) * TILE]

    def slants():
        row = [points_ref[step - 1, k : k + 1, :] for k in range(7)]
        weight = row[6]
        heads = jnp.dot(out_ref[...], jets[...], preferred_element_type=F32)
        table = [[heads[i : i + 1, k * slots : (k + 1) * slots] for i in range(4)] for k in range(5)]
        table[0] = [table[0][i] + bias_ref[0:1, i : i + 1] for i in range(4)]
        _, pull = jax.vjp(lambda t: point_loss(t, row[1], row[3:6], weight), table)
        (slant,) = pull(jnp.ones_like(weight))
        at = lax.broadcasted_iota(jnp.int32, (16, slots), 0)
        pieces = []
        for k in range(5):
            piece = jnp.zeros((16, slots), F32)
            for i in range(4):
                piece = jnp.where(at == i, slant[k][i], piece)
            if k == 0:
                piece = jnp.where(at == 4, weight, piece)
                piece = jnp.where(at == 5, F32(1.0), piece)
            pieces.append(piece)
        cot = jnp.concatenate(pieces, 1)
        scaled[0:16, :] = cot.astype(BF16)
        small_ref[8:16, 0:8] += lax.dot_general(
            cot[0:8],
            cot[0:8],
            ROWS_DOT,
            precision=lax.Precision.HIGHEST,
            preferred_element_type=F32,
        )

    @pl.when(step == 0)
    def _():
        pl.semaphore_signal(barrier, inc=1, device_id={"dp": other}, device_id_type=MESH)
        gram_ref[...] = jnp.zeros_like(gram_ref)
        small_ref[...] = jnp.zeros_like(small_ref)
        for part in range(tiles):
            first_jet(part)

        hidden_jets()

    @pl.when((step > 0) & (step < pairs))
    def _():
        slants()
        for part in range(tiles):
            gram_rows(tiles - 1 - part)
            first_jet(part)
        hidden_jets()

    @pl.when(step == pairs)
    def _():
        slants()
        copies = []

        def send(at, source, target):
            copy = pltpu.make_async_remote_copy(
                src_ref=source,
                dst_ref=target,
                send_sem=send_sem.at[at],
                recv_sem=recv_sem.at[at],
                device_id={"dp": other},
                device_id_type=MESH,
            )
            copy.start()
            copies.append((copy, source, target))

        pl.semaphore_wait(barrier, 1)
        for i in reversed(range(tiles)):
            gram_rows(i)
            block = i * tiles - i * (i - 1) // 2
            for j in range(tiles - i):
                send(block + j, gram_ref.at[block + j], gram_b.at[block + j])
        send(gram_ref.shape[0], small_ref, small_b)
        for copy, source, target in copies:
            copy.wait()
            source[...] += target[...]


def solve_rows(own_rows, gram_ref, small_ref, inverse_ref, update_ref, full, high):
    width = full.shape[0]
    tiles = width // TILE
    first_row = pl.multiple_of(lax.axis_index("dp") * own_rows, own_rows)
    small = small_ref[...]
    weight_sum = small[12:13, 5:6]
    share = 1.0 / weight_sum
    sums = [jnp.zeros((1, TILE), F32) for _ in range(tiles)]
    here = lax.broadcasted_iota(jnp.int32, (TILE, TILE), 0)
    there = lax.broadcasted_iota(jnp.int32, (TILE, TILE), 1)
    damp = jnp.where(here == there, F32(DAMP_FACTOR), F32(0.0))
    block = 0
    for i in range(tiles):
        for j in range(i, tiles):
            piece = gram_ref[block] * share
            block += 1
            if i == j:
                piece = piece + damp
            turned = piece.T
            rows, cols = slice(i * TILE, (i + 1) * TILE), slice(j * TILE, (j + 1) * TILE)
            full[rows, cols] = piece
            high[0, rows, cols] = piece.astype(BF16)
            sums[i] = sums[i] + jnp.sum(jnp.abs(turned), 0, keepdims=True)
            if i != j:
                full[cols, rows] = turned
                high[0, cols, rows] = turned.astype(BF16)
                sums[j] = sums[j] + jnp.sum(jnp.abs(piece), 0, keepdims=True)
    largest = functools.reduce(jnp.maximum, sums)
    shrink = 1.0 / jnp.max(largest, 1, keepdims=True)
    mine = full[pl.ds(first_row, own_rows), :]
    at_row = lax.broadcasted_iota(jnp.int32, mine.shape, 0) + first_row
    at_col = lax.broadcasted_iota(jnp.int32, mine.shape, 1)
    iterate = jnp.where(at_row == at_col, F32(2.0), F32(0.0)) - mine * shrink

    def split(value):
        upper = value.astype(BF16)
        return upper, (value - upper.astype(F32)).astype(BF16)

    def times(value, at):
        both = jnp.concatenate(split(value), 0)
        both = jnp.dot(both, high[at, 0:width, :], preferred_element_type=F32)
        return both[:own_rows] + both[own_rows:]

    at = 0
    for turn in range(ITERS - 2):
        if turn > 0:
            upper, lower = split(iterate)
            high[at, width : width + own_rows, :] = upper
            high[at, width + own_rows : width + 2 * own_rows, :] = lower
        reach = width + 2 * own_rows if turn > 0 else width
        products = []
        for j in range(tiles):
            cols = slice(j * TILE, (j + 1) * TILE)
            square = jnp.dot(
                high[at, 0:reach, :], high[at, 0:width, cols], preferred_element_type=F32
            )
            if turn == 0:
                later = shrink * (2.0 * full[:, cols] - shrink * square)
            else:
                later = 2.0 * full[:, cols] - square[0:width]
                products.append(
                    square[width : width + own_rows] + square[width + own_rows :]
                )
            full[:, cols] = later
            high[1 - at, 0:width, cols] = later.astype(BF16)
        if turn > 0:
            iterate = 2.0 * iterate - jnp.concatenate(products, 1)
        at = 1 - at
    iterate = 2.0 * iterate - times(iterate, at)
    turned = iterate - times(iterate, at)
    turned = turned - times(turned, at)
    iterate = (iterate + turned) * shrink
    inverse_ref[...] = iterate
    merged = lax.dot_general(
        small[0:8, :] / weight_sum,
        iterate,
        ROWS_DOT,
        precision=lax.Precision.HIGHEST,
        preferred_element_type=F32,
    )
    outer = [[small[8 + i : 9 + i, j : j + 1] for j in range(4)] for i in range(4)]
    trace = outer[0][0] + outer[1][1] + outer[2][2] + outer[3][3]
    lower = [[None] * 4 for _ in range(4)]
    for i in range(4):
        for j in range(i + 1):
            entry = 4.0 * outer[i][j] / trace
            if i == j:
                entry = entry + DAMP_OUTPUT
            for k in range(j):
                entry = entry - lower[i][k] * lower[j][k]
            lower[i][j] = jnp.sqrt(entry) if i == j else entry / lower[j][j]
    solved = [merged[i : i + 1, :] for i in range(4)]
    for i in range(4):
        for k in range(i):
            solved[i] = solved[i] - lower[i][k] * solved[k]
        solved[i] = solved[i] / lower[i][i]
    for i in reversed(range(4)):
        for k in range(i + 1, 4):
            solved[i] = solved[i] - lower[k][i] * solved[k]
        solved[i] = solved[i] / lower[i][i]
    at = lax.broadcasted_iota(jnp.int32, (4, own_rows), 0)
    update = jnp.zeros((4, own_rows), F32)
    for i in range(4):
        update = jnp.where(at == i, solved[i], update)
    update_ref[...] = update


def on_device(coords, forcing, bins, counts, bin_weight, w_in, b_in, w_mid, b_mid, w_out, b_out):
    slots = coords.shape[1]
    width = w_mid.shape[0]
    size = lax.axis_size("dp")
    half = size // 2
    pairs = half // 2
    tiles = width // TILE
    blocks = tiles * (tiles + 1) // 2
    own_rows = width // size
    points, cols, mid = pl.pallas_call(
        functools.partial(share_points, size),
        out_shape=(
            jax.ShapeDtypeStruct((pairs, 8, slots), F32),
            jax.ShapeDtypeStruct((width, 8), F32),
            jax.ShapeDtypeStruct((width, width), BF16),
        ),
        in_specs=[VMEM] * 8 + [pl.BlockSpec(memory_space=pl.ANY)],
        out_specs=(VMEM, VMEM, pl.BlockSpec(memory_space=pl.ANY)),
        scratch_shapes=[
            pltpu.VMEM((8, slots), F32),
            pltpu.VMEM((half, 8, slots), F32),
            pltpu.VMEM((width, width), BF16),
            pltpu.VMEM((width, width), BF16),
            pltpu.SemaphoreType.DMA((half,)),
            pltpu.SemaphoreType.DMA((half,)),
            pltpu.SemaphoreType.DMA((2,)),
        ],
        compiler_params=pltpu.CompilerParams(
            collective_id=0, has_side_effects=True, vmem_limit_bytes=BIG
        ),
        name="share_points",
    )(
        coords, forcing, bins[None], counts[None], bin_weight[None], w_in, b_in[None], b_mid[None],
        w_mid,
    )
    fixed = lambda *shape: pl.BlockSpec(shape, lambda i: (0,) * len(shape))
    gram, small = pl.pallas_call(
        point_terms,
        grid=(pairs + 1,),
        out_shape=(
            jax.ShapeDtypeStruct((blocks, TILE, TILE), F32),
            jax.ShapeDtypeStruct((16, width), F32),
        ),
        in_specs=[
            fixed(pairs, 8, slots),
            fixed(width, 8),
            fixed(width, width),
            fixed(4, width),
            fixed(1, 4),
        ],
        out_specs=(fixed(blocks, TILE, TILE), fixed(16, width)),
        scratch_shapes=[
            pltpu.VMEM((width, 5 * slots), BF16),
            pltpu.VMEM((width, 5 * slots), BF16),
            pltpu.VMEM((width + 16, 5 * slots), BF16),
            pltpu.VMEM((blocks, TILE, TILE), F32),
            pltpu.VMEM((16, width), F32),
            pltpu.SemaphoreType.DMA((blocks + 1,)),
            pltpu.SemaphoreType.DMA((blocks + 1,)),
        ],
        compiler_params=pltpu.CompilerParams(
            collective_id=1, has_side_effects=True, vmem_limit_bytes=BIG
        ),
        name="point_terms",
    )(points, cols, mid, w_out.T, b_out[None])
    inverse, update = pl.pallas_call(
        functools.partial(solve_rows, own_rows),
        out_shape=(
            jax.ShapeDtypeStruct((own_rows, width), F32),
            jax.ShapeDtypeStruct((4, own_rows), F32),
        ),
        in_specs=[VMEM, VMEM],
        out_specs=(VMEM, VMEM),
        scratch_shapes=[
            pltpu.VMEM((width, width), F32),
            pltpu.VMEM((2, width + 2 * own_rows, width), BF16),
        ],
        compiler_params=pltpu.CompilerParams(vmem_limit_bytes=BIG),
        name="solve_rows",
    )(gram, small)
    return (update.T, inverse)


def solution(mesh):
    placed = (
        P(None, ("groups", "dp")),
        P(None, ("groups", "dp")),
        P(("groups", "dp")),
        P(("groups", "dp")),
        P("groups"),
        P("groups", None),
        P("groups"),
        P("groups", None),
        P("groups"),
        P("groups", None),
        P("groups"),
    )
    return jax.shard_map(
        on_device,
        mesh=mesh,
        in_specs=placed,
        out_specs=(P(("groups", "dp"), None), P(("groups", "dp"), None)),
        check_vma=False,
    )
```

```python
import functools

import jax
import jax.numpy as jnp
from jax import lax
from jax.experimental import pallas as pl
from jax.experimental.pallas import tpu as pltpu
from jax.sharding import PartitionSpec as P

ITERS = 6
VISCOSITY = 0.05
DAMP_FACTOR = 1.0
DAMP_OUTPUT = 0.1

TILE = 256
MESH = pl.DeviceIdType.MESH
VMEM = pl.BlockSpec(memory_space=pltpu.VMEM)
BIG = 56 * 1024 * 1024
ROWS_DOT = (((1,), (1,)), ((), ()))
F32 = jnp.float32
BF16 = jnp.bfloat16


def share_points(
    axis_size, coords_ref, forcing_ref, bins_ref, count_ref, level_ref, w_in_ref, b_in_ref, b_mid_ref,
    mid_ref, out_ref, cols_ref, mid_out, own, held, plain, turned, send_sem, recv_sem, local_sem,
):
    half = axis_size // 2
    me = lax.axis_index("dp")
    place = me // 2
    parity = me % 2
    slots = coords_ref.shape[1]
    width = mid_ref.shape[0]
    tiles = width // TILE
    fetch = pltpu.make_async_copy(mid_ref, plain, local_sem.at[0])
    fetch.start()
    barrier = pltpu.get_barrier_semaphore()
    for hop in range(1, half):
        other = (place + hop) % half
        pl.semaphore_signal(
            barrier, inc=1, device_id={"dp": other * 2 + parity}, device_id_type=MESH
        )
    bins = bins_ref[...]
    weight = jnp.zeros((1, slots), F32)
    for level in range(level_ref.shape[1]):
        weight = jnp.where(bins == level, level_ref[0:1, level : level + 1], weight)
    at = lax.broadcasted_iota(jnp.int32, (8, slots), 0)
    every = jnp.zeros((8, slots), F32)
    for k in range(3):
        every = jnp.where(at == k, coords_ref[k : k + 1, :], every)
        every = jnp.where(at == 3 + k, forcing_ref[k : k + 1, :], every)
    every = jnp.where(at == 6, weight, every)
    slot = lax.broadcasted_iota(jnp.int32, (8, slots), 1)
    every = jnp.where(slot < count_ref[0:1, 0:1], every, F32(0.0))
    source = lax.broadcasted_iota(jnp.int32, (slots, slots), 0)
    target = lax.broadcasted_iota(jnp.int32, (slots, slots), 1)
    target = jnp.where(me >= half, slots - 1 - target, target)
    move = jnp.where(source == target, F32(1.0), F32(0.0))
    own[...] = jnp.dot(
        every, move, precision=lax.Precision.HIGHEST, preferred_element_type=F32
    )
    pl.semaphore_wait(barrier, half - 1)
    copies = []
    for hop in range(1, half):
        other = (place + hop) % half
        copy = pltpu.make_async_remote_copy(
            src_ref=own,
            dst_ref=held.at[place],
            send_sem=send_sem.at[hop],
            recv_sem=recv_sem.at[place],
            device_id={"dp": other * 2 + parity},
            device_id_type=MESH,
        )
        copy.start()
        copies.append(copy)
    held[place] = own[...]
    table = jnp.zeros((8, width), F32)
    at = lax.broadcasted_iota(jnp.int32, (8, width), 0)
    for k in range(3):
        table = jnp.where(at == k, w_in_ref[k : k + 1, :], table)
    table = jnp.where(at == 3, b_in_ref[...], table)
    table = jnp.where(at == 4, b_mid_ref[...], table)
    cols_ref[...] = table.T
    fetch.wait()
    for i in range(tiles):
        for j in range(tiles):
            turned[j * TILE : (j + 1) * TILE, i * TILE : (i + 1) * TILE] = plain[
                i * TILE : (i + 1) * TILE, j * TILE : (j + 1) * TILE
            ].T
    give = pltpu.make_async_copy(turned, mid_out, local_sem.at[1])
    give.start()
    for hop in range(1, half):
        other = (place + hop) % half
        pltpu.make_async_remote_copy(
            src_ref=own,
            dst_ref=held.at[other],
            send_sem=send_sem.at[hop],
            recv_sem=recv_sem.at[other],
            device_id={"dp": other * 2 + parity},
            device_id_type=MESH,
        ).wait_recv()
    for pair in range(half // 2):
        out_ref[pair] = held[pair] + held[pair + half // 2]
    for copy in copies:
        copy.wait_send()
    give.wait()


def point_loss(heads, height, pushes, weight):
    value, slopes, curve = heads[0], heads[1:4], heads[4]
    wall = 1.0 - height * height
    wall_slope = -2.0 * height
    vel = [wall * value[i] for i in range(3)]
    vel_slope = [[wall * slopes[k][i] for i in range(3)] for k in range(3)]
    for i in range(3):
        vel_slope[1][i] = wall_slope * value[i] + vel_slope[1][i]
    total = vel_slope[0][0] + vel_slope[1][1] + vel_slope[2][2]
    total = total * total
    for i in range(3):
        lap = -2.0 * value[i] + 2.0 * (wall_slope * slopes[1][i]) + wall * curve[i]
        convect = vel[0] * vel_slope[0][i] + vel[1] * vel_slope[1][i] + vel[2] * vel_slope[2][i]
        momentum = convect + slopes[i][3] - VISCOSITY * lap - pushes[i]
        total = total + momentum * momentum
    return 0.5 * (weight * total)


def point_terms(points_ref, cols_ref, mid_ref, out_ref, bias_ref, gram_ref, small_ref, first, jets, scaled, gram_b, small_b, send_sem, recv_sem):
    width = mid_ref.shape[0]
    pairs, _, slots = points_ref.shape
    tiles = width // TILE
    step = pl.program_id(0)
    me = lax.axis_index("dp")
    other = me + 1 - 2 * (me % 2)
    barrier = pltpu.get_barrier_semaphore()

    def column(part, k):
        return cols_ref[part * TILE : (part + 1) * TILE, k : k + 1]

    def first_jet(part):
        row = [points_ref[step, k : k + 1, :] for k in range(3)]
        rows = slice(part * TILE, (part + 1) * TILE)
        w = [column(part, k) for k in range(3)]
        pre = row[0] * w[0] + row[1] * w[1] + row[2] * w[2] + column(part, 3)
        act = jnp.tanh(pre)
        slope = 1.0 - act * act
        curve_in = -2.0 * (w[0] * w[0] + w[1] * w[1] + w[2] * w[2])
        first[rows, 0:slots] = act.astype(BF16)
        for k in range(3):
            first[rows, (k + 1) * slots : (k + 2) * slots] = (slope * w[k]).astype(BF16)
        first[rows, 4 * slots : 5 * slots] = (act * slope * curve_in).astype(BF16)

    def hidden_mixed(part, k):
        rows = slice(part * TILE, (part + 1) * TILE)
        return jnp.dot(
            mid_ref[rows, :], first[:, k * slots : (k + 1) * slots], preferred_element_type=F32
        )

    def keep_jet(part, k, jet):
        weight = points_ref[step, 6:7, :]
        places = slice(k * slots, (k + 1) * slots)
        jets[part * TILE : (part + 1) * TILE, places] = jet.astype(BF16)
        scaled[16 + part * TILE : 16 + (part + 1) * TILE, places] = (jet * weight).astype(BF16)

    def hidden_jets():
        mixed = [hidden_mixed(0, k) for k in range(5)]
        for part in range(tiles):
            later = []
            for k in range(5):
                if part + 1 < tiles:
                    later.append(hidden_mixed(part + 1, k))
                if k == 0:
                    act = jnp.tanh(mixed[0] + column(part, 4))
                    slope = 1.0 - act * act
                    jet = act
                elif k < 4:
                    square = mixed[k] * mixed[k]
                    squares = square if k == 1 else squares + square
                    jet = slope * mixed[k]
                else:
                    jet = slope * (mixed[4] - 2.0 * act * squares)
                keep_jet(part, k, jet)
            mixed = later

    def gram_rows(i):
        start = 0 if i == 0 else 16 + i * TILE
        part = lax.dot_general(
            scaled[start : 16 + (i + 1) * TILE, :],
            jets[i * TILE :, :],
            ROWS_DOT,
            preferred_element_type=F32,
        )
        if i == 0:
            small_ref[0:8, :] += part[0:8, :]
            part = part[16:, :]
        block = i * tiles - i * (i - 1) // 2
        for j in range(tiles - i):
            gram_ref[block + j] += part[:, j * TILE : (j + 1) * TILE]

    def slants():
        row = [points_ref[step - 1, k : k + 1, :] for k in range(7)]
        weight = row[6]
        heads = jnp.dot(out_ref[...], jets[...], preferred_element_type=F32)
        table = [[heads[i : i + 1, k * slots : (k + 1) * slots] for i in range(4)] for k in range(5)]
        table[0] = [table[0][i] + bias_ref[0:1, i : i + 1] for i in range(4)]
        _, pull = jax.vjp(lambda t: point_loss(t, row[1], row[3:6], weight), table)
        (slant,) = pull(jnp.ones_like(weight))
        at = lax.broadcasted_iota(jnp.int32, (16, slots), 0)
        pieces = []
        for k in range(5):
            piece = jnp.zeros((16, slots), F32)
            for i in range(4):
                piece = jnp.where(at == i, slant[k][i], piece)
            if k == 0:
                piece = jnp.where(at == 4, weight, piece)
                piece = jnp.where(at == 5, F32(1.0), piece)
            pieces.append(piece)
        cot = jnp.concatenate(pieces, 1)
        scaled[0:16, :] = cot.astype(BF16)
        small_ref[8:16, 0:8] += lax.dot_general(
            cot[0:8],
            cot[0:8],
            ROWS_DOT,
            precision=lax.Precision.HIGHEST,
            preferred_element_type=F32,
        )

    @pl.when(step == 0)
    def _():
        pl.semaphore_signal(barrier, inc=1, device_id={"dp": other}, device_id_type=MESH)
        gram_ref[...] = jnp.zeros_like(gram_ref)
        small_ref[...] = jnp.zeros_like(small_ref)
        for part in range(tiles):
            first_jet(part)

        hidden_jets()

    @pl.when((step > 0) & (step < pairs))
    def _():
        slants()
        for part in range(tiles):
            gram_rows(tiles - 1 - part)
            first_jet(part)
        hidden_jets()

    @pl.when(step == pairs)
    def _():
        slants()
        copies = []

        def send(at, source, target):
            copy = pltpu.make_async_remote_copy(
                src_ref=source,
                dst_ref=target,
                send_sem=send_sem.at[at],
                recv_sem=recv_sem.at[at],
                device_id={"dp": other},
                device_id_type=MESH,
            )
            copy.start()
            copies.append((copy, source, target))

        pl.semaphore_wait(barrier, 1)
        for i in reversed(range(tiles)):
            gram_rows(i)
            block = i * tiles - i * (i - 1) // 2
            for j in range(tiles - i):
                send(block + j, gram_ref.at[block + j], gram_b.at[block + j])
        send(gram_ref.shape[0], small_ref, small_b)
        for copy, source, target in copies:
            copy.wait()
            source[...] += target[...]


def solve_rows(own_rows, gram_ref, small_ref, inverse_ref, update_ref, full, high):
    width = full.shape[0]
    tiles = width // TILE
    lead = 2 * own_rows
    first_row = pl.multiple_of(lax.axis_index("dp") * own_rows, own_rows)
    small = small_ref[...]
    weight_sum = small[12:13, 5:6]
    share = 1.0 / weight_sum
    sums = [jnp.zeros((1, TILE), F32) for _ in range(tiles)]
    here = lax.broadcasted_iota(jnp.int32, (TILE, TILE), 0)
    there = lax.broadcasted_iota(jnp.int32, (TILE, TILE), 1)
    damp = jnp.where(here == there, F32(DAMP_FACTOR), F32(0.0))
    block = 0
    for i in range(tiles):
        for j in range(i, tiles):
            piece = gram_ref[block] * share
            block += 1
            if i == j:
                piece = piece + damp
            turned = piece.T
            rows, cols = slice(i * TILE, (i + 1) * TILE), slice(j * TILE, (j + 1) * TILE)
            full[rows, cols] = piece
            high[0, lead + rows.start : lead + rows.stop, cols] = piece.astype(BF16)
            sums[i] = sums[i] + jnp.sum(jnp.abs(turned), 0, keepdims=True)
            if i != j:
                full[cols, rows] = turned
                high[0, lead + cols.start : lead + cols.stop, rows] = turned.astype(BF16)
                sums[j] = sums[j] + jnp.sum(jnp.abs(piece), 0, keepdims=True)
    largest = functools.reduce(jnp.maximum, sums)
    shrink = 1.0 / jnp.max(largest, 1, keepdims=True)
    mine = full[pl.ds(first_row, own_rows), :]
    at_row = lax.broadcasted_iota(jnp.int32, mine.shape, 0) + first_row
    at_col = lax.broadcasted_iota(jnp.int32, mine.shape, 1)
    iterate = jnp.where(at_row == at_col, F32(2.0), F32(0.0)) - mine * shrink

    def split(value):
        upper = value.astype(BF16)
        return upper, (value - upper.astype(F32)).astype(BF16)

    def times(value, at):
        both = jnp.concatenate(split(value), 0)
        both = jnp.dot(both, high[at, lead:, :], preferred_element_type=F32)
        return both[:own_rows] + both[own_rows:]

    at = 0
    for turn in range(ITERS - 2):
        if turn > 0:
            upper, lower = split(iterate)
            high[at, 0:own_rows, :] = upper
            high[at, own_rows:lead, :] = lower
        start = 0 if turn > 0 else lead
        products = [None] * tiles
        for j in reversed(range(tiles)):
            cols = slice(j * TILE, (j + 1) * TILE)
            reach = (j + 1) * TILE
            square = jnp.dot(
                high[at, start : lead + reach, :], high[at, lead:, cols], preferred_element_type=F32
            )
            if turn == 0:
                later = shrink * (2.0 * full[0:reach, cols] - shrink * square)
            else:
                products[j] = square[0:own_rows] + square[own_rows:lead]
                later = 2.0 * full[0:reach, cols] - square[lead:]
            full[0:reach, cols] = later
            half = later.astype(BF16)
            high[1 - at, lead : lead + reach, cols] = half
            for i in range(j):
                high[1 - at, lead + cols.start : lead + cols.stop, i * TILE : (i + 1) * TILE] = half[
                    i * TILE : (i + 1) * TILE
                ].T
        if turn > 0:
            iterate = 2.0 * iterate - jnp.concatenate(products, 1)
        at = 1 - at
    iterate = 2.0 * iterate - times(iterate, at)
    turned = iterate - times(iterate, at)
    turned = turned - times(turned, at)
    iterate = (iterate + turned) * shrink
    inverse_ref[...] = iterate
    merged = lax.dot_general(
        small[0:8, :] / weight_sum,
        iterate,
        ROWS_DOT,
        precision=lax.Precision.HIGHEST,
        preferred_element_type=F32,
    )
    outer = [[small[8 + i : 9 + i, j : j + 1] for j in range(4)] for i in range(4)]
    trace = outer[0][0] + outer[1][1] + outer[2][2] + outer[3][3]
    lower = [[None] * 4 for _ in range(4)]
    for i in range(4):
        for j in range(i + 1):
            entry = 4.0 * outer[i][j] / trace
            if i == j:
                entry = entry + DAMP_OUTPUT
            for k in range(j):
                entry = entry - lower[i][k] * lower[j][k]
            lower[i][j] = jnp.sqrt(entry) if i == j else entry / lower[j][j]
    solved = [merged[i : i + 1, :] for i in range(4)]
    for i in range(4):
        for k in range(i):
            solved[i] = solved[i] - lower[i][k] * solved[k]
        solved[i] = solved[i] / lower[i][i]
    for i in reversed(range(4)):
        for k in range(i + 1, 4):
            solved[i] = solved[i] - lower[k][i] * solved[k]
        solved[i] = solved[i] / lower[i][i]
    at = lax.broadcasted_iota(jnp.int32, (4, own_rows), 0)
    update = jnp.zeros((4, own_rows), F32)
    for i in range(4):
        update = jnp.where(at == i, solved[i], update)
    update_ref[...] = update


def on_device(coords, forcing, bins, counts, bin_weight, w_in, b_in, w_mid, b_mid, w_out, b_out):
    slots = coords.shape[1]
    width = w_mid.shape[0]
    size = lax.axis_size("dp")
    half = size // 2
    pairs = half // 2
    tiles = width // TILE
    blocks = tiles * (tiles + 1) // 2
    own_rows = width // size
    points, cols, mid = pl.pallas_call(
        functools.partial(share_points, size),
        out_shape=(
            jax.ShapeDtypeStruct((pairs, 8, slots), F32),
            jax.ShapeDtypeStruct((width, 8), F32),
            jax.ShapeDtypeStruct((width, width), BF16),
        ),
        in_specs=[VMEM] * 8 + [pl.BlockSpec(memory_space=pl.ANY)],
        out_specs=(VMEM, VMEM, pl.BlockSpec(memory_space=pl.ANY)),
        scratch_shapes=[
            pltpu.VMEM((8, slots), F32),
            pltpu.VMEM((half, 8, slots), F32),
            pltpu.VMEM((width, width), BF16),
            pltpu.VMEM((width, width), BF16),
            pltpu.SemaphoreType.DMA((half,)),
            pltpu.SemaphoreType.DMA((half,)),
            pltpu.SemaphoreType.DMA((2,)),
        ],
        compiler_params=pltpu.CompilerParams(
            collective_id=0, has_side_effects=True, vmem_limit_bytes=BIG
        ),
        name="share_points",
    )(
        coords, forcing, bins[None], counts[None], bin_weight[None], w_in, b_in[None], b_mid[None],
        w_mid,
    )
    fixed = lambda *shape: pl.BlockSpec(shape, lambda i: (0,) * len(shape))
    gram, small = pl.pallas_call(
        point_terms,
        grid=(pairs + 1,),
        out_shape=(
            jax.ShapeDtypeStruct((blocks, TILE, TILE), F32),
            jax.ShapeDtypeStruct((16, width), F32),
        ),
        in_specs=[
            fixed(pairs, 8, slots),
            fixed(width, 8),
            fixed(width, width),
            fixed(4, width),
            fixed(1, 4),
        ],
        out_specs=(fixed(blocks, TILE, TILE), fixed(16, width)),
        scratch_shapes=[
            pltpu.VMEM((width, 5 * slots), BF16),
            pltpu.VMEM((width, 5 * slots), BF16),
            pltpu.VMEM((width + 16, 5 * slots), BF16),
            pltpu.VMEM((blocks, TILE, TILE), F32),
            pltpu.VMEM((16, width), F32),
            pltpu.SemaphoreType.DMA((blocks + 1,)),
            pltpu.SemaphoreType.DMA((blocks + 1,)),
        ],
        compiler_params=pltpu.CompilerParams(
            collective_id=1, has_side_effects=True, vmem_limit_bytes=BIG
        ),
        name="point_terms",
    )(points, cols, mid, w_out.T, b_out[None])
    inverse, update = pl.pallas_call(
        functools.partial(solve_rows, own_rows),
        out_shape=(
            jax.ShapeDtypeStruct((own_rows, width), F32),
            jax.ShapeDtypeStruct((4, own_rows), F32),
        ),
        in_specs=[VMEM, VMEM],
        out_specs=(VMEM, VMEM),
        scratch_shapes=[
            pltpu.VMEM((width, width), F32),
            pltpu.VMEM((2, width + 2 * own_rows, width), BF16),
        ],
        compiler_params=pltpu.CompilerParams(vmem_limit_bytes=BIG),
        name="solve_rows",
    )(gram, small)
    return (update.T, inverse)


def solution(mesh):
    placed = (
        P(None, ("groups", "dp")),
        P(None, ("groups", "dp")),
        P(("groups", "dp")),
        P(("groups", "dp")),
        P("groups"),
        P("groups", None),
        P("groups"),
        P("groups", None),
        P("groups"),
        P("groups", None),
        P("groups"),
    )
    return jax.shard_map(
        on_device,
        mesh=mesh,
        in_specs=placed,
        out_specs=(P(("groups", "dp"), None), P(("groups", "dp"), None)),
        check_vma=False,
    )
```

```python
import functools

import jax
import jax.numpy as jnp
from jax import lax
from jax.experimental import pallas as pl
from jax.experimental.pallas import tpu as pltpu
from jax.sharding import PartitionSpec as P

ITERS = 6
VISCOSITY = 0.05
DAMP_FACTOR = 1.0
DAMP_OUTPUT = 0.1

TILE = 256
MESH = pl.DeviceIdType.MESH
VMEM = pl.BlockSpec(memory_space=pltpu.VMEM)
BIG = 56 * 1024 * 1024
ROWS_DOT = (((1,), (1,)), ((), ()))
F32 = jnp.float32
BF16 = jnp.bfloat16


def share_points(
    axis_size, coords_ref, forcing_ref, bins_ref, count_ref, level_ref, w_in_ref, b_in_ref, b_mid_ref,
    mid_ref, out_ref, cols_ref, mid_out, own, held, plain, turned, send_sem, recv_sem, local_sem,
):
    half = axis_size // 2
    me = lax.axis_index("dp")
    place = me // 2
    parity = me % 2
    slots = coords_ref.shape[1]
    width = mid_ref.shape[0]
    tiles = width // TILE
    fetch = pltpu.make_async_copy(mid_ref, plain, local_sem.at[0])
    fetch.start()
    barrier = pltpu.get_barrier_semaphore()
    for hop in range(1, half):
        other = (place + hop) % half
        pl.semaphore_signal(
            barrier, inc=1, device_id={"dp": other * 2 + parity}, device_id_type=MESH
        )
    bins = bins_ref[...]
    weight = jnp.zeros((1, slots), F32)
    for level in range(level_ref.shape[1]):
        weight = jnp.where(bins == level, level_ref[0:1, level : level + 1], weight)
    at = lax.broadcasted_iota(jnp.int32, (8, slots), 0)
    every = jnp.zeros((8, slots), F32)
    for k in range(3):
        every = jnp.where(at == k, coords_ref[k : k + 1, :], every)
        every = jnp.where(at == 3 + k, forcing_ref[k : k + 1, :], every)
    every = jnp.where(at == 6, weight, every)
    slot = lax.broadcasted_iota(jnp.int32, (8, slots), 1)
    every = jnp.where(slot < count_ref[0:1, 0:1], every, F32(0.0))
    source = lax.broadcasted_iota(jnp.int32, (slots, slots), 0)
    target = lax.broadcasted_iota(jnp.int32, (slots, slots), 1)
    target = jnp.where(me >= half, slots - 1 - target, target)
    move = jnp.where(source == target, F32(1.0), F32(0.0))
    own[...] = jnp.dot(
        every, move, precision=lax.Precision.HIGHEST, preferred_element_type=F32
    )
    pl.semaphore_wait(barrier, half - 1)
    copies = []
    for hop in range(1, half):
        other = (place + hop) % half
        copy = pltpu.make_async_remote_copy(
            src_ref=own,
            dst_ref=held.at[place],
            send_sem=send_sem.at[hop],
            recv_sem=recv_sem.at[place],
            device_id={"dp": other * 2 + parity},
            device_id_type=MESH,
        )
        copy.start()
        copies.append(copy)
    held[place] = own[...]
    table = jnp.zeros((8, width), F32)
    at = lax.broadcasted_iota(jnp.int32, (8, width), 0)
    for k in range(3):
        table = jnp.where(at == k, w_in_ref[k : k + 1, :], table)
    table = jnp.where(at == 3, b_in_ref[...], table)
    table = jnp.where(at == 4, b_mid_ref[...], table)
    cols_ref[...] = table.T
    fetch.wait()
    for i in range(tiles):
        for j in range(tiles):
            turned[j * TILE : (j + 1) * TILE, i * TILE : (i + 1) * TILE] = plain[
                i * TILE : (i + 1) * TILE, j * TILE : (j + 1) * TILE
            ].T
    give = pltpu.make_async_copy(turned, mid_out, local_sem.at[1])
    give.start()
    for hop in range(1, half):
        other = (place + hop) % half
        pltpu.make_async_remote_copy(
            src_ref=own,
            dst_ref=held.at[other],
            send_sem=send_sem.at[hop],
            recv_sem=recv_sem.at[other],
            device_id={"dp": other * 2 + parity},
            device_id_type=MESH,
        ).wait_recv()
    for pair in range(half // 2):
        out_ref[pair] = held[pair] + held[pair + half // 2]
    for copy in copies:
        copy.wait_send()
    give.wait()


def point_loss(heads, height, pushes, weight):
    value, slopes, curve = heads[0], heads[1:4], heads[4]
    wall = 1.0 - height * height
    wall_slope = -2.0 * height
    vel = [wall * value[i] for i in range(3)]
    vel_slope = [[wall * slopes[k][i] for i in range(3)] for k in range(3)]
    for i in range(3):
        vel_slope[1][i] = wall_slope * value[i] + vel_slope[1][i]
    total = vel_slope[0][0] + vel_slope[1][1] + vel_slope[2][2]
    total = total * total
    for i in range(3):
        lap = -2.0 * value[i] + 2.0 * (wall_slope * slopes[1][i]) + wall * curve[i]
        convect = vel[0] * vel_slope[0][i] + vel[1] * vel_slope[1][i] + vel[2] * vel_slope[2][i]
        momentum = convect + slopes[i][3] - VISCOSITY * lap - pushes[i]
        total = total + momentum * momentum
    return 0.5 * (weight * total)


def point_terms(points_ref, cols_ref, mid_ref, out_ref, bias_ref, gram_ref, small_ref, first, jets, scaled, gram_b, small_b, send_sem, recv_sem):
    width = mid_ref.shape[0]
    pairs, _, slots = points_ref.shape
    tiles = width // TILE
    step = pl.program_id(0)
    me = lax.axis_index("dp")
    other = me + 1 - 2 * (me % 2)
    barrier = pltpu.get_barrier_semaphore()

    def column(part, k):
        return cols_ref[part * TILE : (part + 1) * TILE, k : k + 1]

    def first_jet(part):
        row = [points_ref[step, k : k + 1, :] for k in range(3)]
        rows = slice(part * TILE, (part + 1) * TILE)
        w = [column(part, k) for k in range(3)]
        pre = row[0] * w[0] + row[1] * w[1] + row[2] * w[2] + column(part, 3)
        act = jnp.tanh(pre)
        slope = 1.0 - act * act
        curve_in = -2.0 * (w[0] * w[0] + w[1] * w[1] + w[2] * w[2])
        first[rows, 0:slots] = act.astype(BF16)
        for k in range(3):
            first[rows, (k + 1) * slots : (k + 2) * slots] = (slope * w[k]).astype(BF16)
        first[rows, 4 * slots : 5 * slots] = (act * slope * curve_in).astype(BF16)

    def hidden_mixed(part, k):
        rows = slice(part * TILE, (part + 1) * TILE)
        return jnp.dot(
            mid_ref[rows, :], first[:, k * slots : (k + 1) * slots], preferred_element_type=F32
        )

    def keep_jet(part, k, jet):
        weight = points_ref[step, 6:7, :]
        places = slice(k * slots, (k + 1) * slots)
        jets[part * TILE : (part + 1) * TILE, places] = jet.astype(BF16)
        scaled[16 + part * TILE : 16 + (part + 1) * TILE, places] = (jet * weight).astype(BF16)

    def hidden_jets():
        mixed = [hidden_mixed(0, k) for k in range(5)]
        for part in range(tiles):
            later = []
            for k in range(5):
                if part + 1 < tiles:
                    later.append(hidden_mixed(part + 1, k))
                if k == 0:
                    act = jnp.tanh(mixed[0] + column(part, 4))
                    slope = 1.0 - act * act
                    jet = act
                elif k < 4:
                    square = mixed[k] * mixed[k]
                    squares = square if k == 1 else squares + square
                    jet = slope * mixed[k]
                else:
                    jet = slope * (mixed[4] - 2.0 * act * squares)
                keep_jet(part, k, jet)
            mixed = later

    def gram_rows(i):
        start = 0 if i == 0 else 16 + i * TILE
        part = lax.dot_general(
            scaled[start : 16 + (i + 1) * TILE, :],
            jets[i * TILE :, :],
            ROWS_DOT,
            preferred_element_type=F32,
        )
        if i == 0:
            small_ref[0:8, :] += part[0:8, :]
            part = part[16:, :]
        block = i * tiles - i * (i - 1) // 2
        for j in range(tiles - i):
            gram_ref[block + j] += part[:, j * TILE : (j + 1) * TILE]

    def slants():
        row = [points_ref[step - 1, k : k + 1, :] for k in range(7)]
        weight = row[6]
        heads = jnp.dot(out_ref[...], jets[...], preferred_element_type=F32)
        table = [[heads[i : i + 1, k * slots : (k + 1) * slots] for i in range(4)] for k in range(5)]
        table[0] = [table[0][i] + bias_ref[0:1, i : i + 1] for i in range(4)]
        _, pull = jax.vjp(lambda t: point_loss(t, row[1], row[3:6], weight), table)
        (slant,) = pull(jnp.ones_like(weight))
        at = lax.broadcasted_iota(jnp.int32, (16, slots), 0)
        pieces = []
        for k in range(5):
            piece = jnp.zeros((16, slots), F32)
            for i in range(4):
                piece = jnp.where(at == i, slant[k][i], piece)
            if k == 0:
                piece = jnp.where(at == 4, weight, piece)
                piece = jnp.where(at == 5, F32(1.0), piece)
            pieces.append(piece)
        cot = jnp.concatenate(pieces, 1)
        scaled[0:16, :] = cot.astype(BF16)
        small_ref[8:16, 0:8] += lax.dot_general(
            cot[0:8],
            cot[0:8],
            ROWS_DOT,
            precision=lax.Precision.HIGHEST,
            preferred_element_type=F32,
        )

    @pl.when(step == 0)
    def _():
        pl.semaphore_signal(barrier, inc=1, device_id={"dp": other}, device_id_type=MESH)
        gram_ref[...] = jnp.zeros_like(gram_ref)
        small_ref[...] = jnp.zeros_like(small_ref)
        for part in range(tiles):
            first_jet(part)

        hidden_jets()

    @pl.when((step > 0) & (step < pairs))
    def _():
        slants()
        for part in range(tiles):
            gram_rows(tiles - 1 - part)
            first_jet(part)
        hidden_jets()

    @pl.when(step == pairs)
    def _():
        copies = []

        def send(at, source, target):
            copy = pltpu.make_async_remote_copy(
                src_ref=source,
                dst_ref=target,
                send_sem=send_sem.at[at],
                recv_sem=recv_sem.at[at],
                device_id={"dp": other},
                device_id_type=MESH,
            )
            copy.start()
            copies.append((copy, source, target))

        pl.semaphore_wait(barrier, 1)
        for i in reversed(range(tiles)):
            if i == 0:
                slants()
            gram_rows(i)
            block = i * tiles - i * (i - 1) // 2
            for j in range(tiles - i):
                send(block + j, gram_ref.at[block + j], gram_b.at[block + j])
        send(gram_ref.shape[0], small_ref, small_b)
        for copy, source, target in copies:
            copy.wait()
            source[...] += target[...]


def solve_rows(own_rows, gram_ref, small_ref, inverse_ref, update_ref, full, high):
    width = full.shape[0]
    tiles = width // TILE
    lead = 2 * own_rows
    first_row = pl.multiple_of(lax.axis_index("dp") * own_rows, own_rows)
    small = small_ref[...]
    weight_sum = small[12:13, 5:6]
    share = 1.0 / weight_sum
    sums = [jnp.zeros((1, TILE), F32) for _ in range(tiles)]
    here = lax.broadcasted_iota(jnp.int32, (TILE, TILE), 0)
    there = lax.broadcasted_iota(jnp.int32, (TILE, TILE), 1)
    damp = jnp.where(here == there, F32(DAMP_FACTOR), F32(0.0))
    block = 0
    for i in range(tiles):
        for j in range(i, tiles):
            piece = gram_ref[block] * share
            block += 1
            if i == j:
                piece = piece + damp
            turned = piece.T
            rows, cols = slice(i * TILE, (i + 1) * TILE), slice(j * TILE, (j + 1) * TILE)
            full[rows, cols] = piece
            high[0, lead + rows.start : lead + rows.stop, cols] = piece.astype(BF16)
            sums[i] = sums[i] + jnp.sum(jnp.abs(turned), 0, keepdims=True)
            if i != j:
                full[cols, rows] = turned
                high[0, lead + cols.start : lead + cols.stop, rows] = turned.astype(BF16)
                sums[j] = sums[j] + jnp.sum(jnp.abs(piece), 0, keepdims=True)
    largest = functools.reduce(jnp.maximum, sums)
    shrink = 1.0 / jnp.max(largest, 1, keepdims=True)
    mine = full[pl.ds(first_row, own_rows), :]
    at_row = lax.broadcasted_iota(jnp.int32, mine.shape, 0) + first_row
    at_col = lax.broadcasted_iota(jnp.int32, mine.shape, 1)
    iterate = jnp.where(at_row == at_col, F32(2.0), F32(0.0)) - mine * shrink

    def split(value):
        upper = value.astype(BF16)
        return upper, (value - upper.astype(F32)).astype(BF16)

    def times(value, at):
        both = jnp.concatenate(split(value), 0)
        both = jnp.dot(both, high[at, lead:, :], preferred_element_type=F32)
        return both[:own_rows] + both[own_rows:]

    at = 0
    for turn in range(ITERS - 2):
        if turn > 0:
            upper, lower = split(iterate)
            high[at, 0:own_rows, :] = upper
            high[at, own_rows:lead, :] = lower
        start = 0 if turn > 0 else lead
        products = [None] * tiles
        for j in reversed(range(tiles)):
            cols = slice(j * TILE, (j + 1) * TILE)
            reach = (j + 1) * TILE
            square = jnp.dot(
                high[at, start : lead + reach, :], high[at, lead:, cols], preferred_element_type=F32
            )
            if turn == 0:
                later = shrink * (2.0 * full[0:reach, cols] - shrink * square)
            else:
                products[j] = square[0:own_rows] + square[own_rows:lead]
                later = 2.0 * full[0:reach, cols] - square[lead:]
            full[0:reach, cols] = later
            half = later.astype(BF16)
            high[1 - at, lead : lead + reach, cols] = half
            for i in range(j):
                high[1 - at, lead + cols.start : lead + cols.stop, i * TILE : (i + 1) * TILE] = half[
                    i * TILE : (i + 1) * TILE
                ].T
        if turn > 0:
            iterate = 2.0 * iterate - jnp.concatenate(products, 1)
        at = 1 - at
    iterate = 2.0 * iterate - times(iterate, at)
    turned = iterate - times(iterate, at)
    turned = turned - times(turned, at)
    iterate = (iterate + turned) * shrink
    inverse_ref[...] = iterate
    merged = lax.dot_general(
        small[0:8, :] / weight_sum,
        iterate,
        ROWS_DOT,
        precision=lax.Precision.HIGHEST,
        preferred_element_type=F32,
    )
    outer = [[small[8 + i : 9 + i, j : j + 1] for j in range(4)] for i in range(4)]
    trace = outer[0][0] + outer[1][1] + outer[2][2] + outer[3][3]
    lower = [[None] * 4 for _ in range(4)]
    for i in range(4):
        for j in range(i + 1):
            entry = 4.0 * outer[i][j] / trace
            if i == j:
                entry = entry + DAMP_OUTPUT
            for k in range(j):
                entry = entry - lower[i][k] * lower[j][k]
            lower[i][j] = jnp.sqrt(entry) if i == j else entry / lower[j][j]
    solved = [merged[i : i + 1, :] for i in range(4)]
    for i in range(4):
        for k in range(i):
            solved[i] = solved[i] - lower[i][k] * solved[k]
        solved[i] = solved[i] / lower[i][i]
    for i in reversed(range(4)):
        for k in range(i + 1, 4):
            solved[i] = solved[i] - lower[k][i] * solved[k]
        solved[i] = solved[i] / lower[i][i]
    at = lax.broadcasted_iota(jnp.int32, (4, own_rows), 0)
    update = jnp.zeros((4, own_rows), F32)
    for i in range(4):
        update = jnp.where(at == i, solved[i], update)
    update_ref[...] = update


def on_device(coords, forcing, bins, counts, bin_weight, w_in, b_in, w_mid, b_mid, w_out, b_out):
    slots = coords.shape[1]
    width = w_mid.shape[0]
    size = lax.axis_size("dp")
    half = size // 2
    pairs = half // 2
    tiles = width // TILE
    blocks = tiles * (tiles + 1) // 2
    own_rows = width // size
    points, cols, mid = pl.pallas_call(
        functools.partial(share_points, size),
        out_shape=(
            jax.ShapeDtypeStruct((pairs, 8, slots), F32),
            jax.ShapeDtypeStruct((width, 8), F32),
            jax.ShapeDtypeStruct((width, width), BF16),
        ),
        in_specs=[VMEM] * 8 + [pl.BlockSpec(memory_space=pl.ANY)],
        out_specs=(VMEM, VMEM, pl.BlockSpec(memory_space=pl.ANY)),
        scratch_shapes=[
            pltpu.VMEM((8, slots), F32),
            pltpu.VMEM((half, 8, slots), F32),
            pltpu.VMEM((width, width), BF16),
            pltpu.VMEM((width, width), BF16),
            pltpu.SemaphoreType.DMA((half,)),
            pltpu.SemaphoreType.DMA((half,)),
            pltpu.SemaphoreType.DMA((2,)),
        ],
        compiler_params=pltpu.CompilerParams(
            collective_id=0, has_side_effects=True, vmem_limit_bytes=BIG
        ),
        name="share_points",
    )(
        coords, forcing, bins[None], counts[None], bin_weight[None], w_in, b_in[None], b_mid[None],
        w_mid,
    )
    fixed = lambda *shape: pl.BlockSpec(shape, lambda i: (0,) * len(shape))
    gram, small = pl.pallas_call(
        point_terms,
        grid=(pairs + 1,),
        out_shape=(
            jax.ShapeDtypeStruct((blocks, TILE, TILE), F32),
            jax.ShapeDtypeStruct((16, width), F32),
        ),
        in_specs=[
            fixed(pairs, 8, slots),
            fixed(width, 8),
            fixed(width, width),
            fixed(4, width),
            fixed(1, 4),
        ],
        out_specs=(fixed(blocks, TILE, TILE), fixed(16, width)),
        scratch_shapes=[
            pltpu.VMEM((width, 5 * slots), BF16),
            pltpu.VMEM((width, 5 * slots), BF16),
            pltpu.VMEM((width + 16, 5 * slots), BF16),
            pltpu.VMEM((blocks, TILE, TILE), F32),
            pltpu.VMEM((16, width), F32),
            pltpu.SemaphoreType.DMA((blocks + 1,)),
            pltpu.SemaphoreType.DMA((blocks + 1,)),
        ],
        compiler_params=pltpu.CompilerParams(
            collective_id=1, has_side_effects=True, vmem_limit_bytes=BIG
        ),
        name="point_terms",
    )(points, cols, mid, w_out.T, b_out[None])
    inverse, update = pl.pallas_call(
        functools.partial(solve_rows, own_rows),
        out_shape=(
            jax.ShapeDtypeStruct((own_rows, width), F32),
            jax.ShapeDtypeStruct((4, own_rows), F32),
        ),
        in_specs=[VMEM, VMEM],
        out_specs=(VMEM, VMEM),
        scratch_shapes=[
            pltpu.VMEM((width, width), F32),
            pltpu.VMEM((2, width + 2 * own_rows, width), BF16),
        ],
        compiler_params=pltpu.CompilerParams(vmem_limit_bytes=BIG),
        name="solve_rows",
    )(gram, small)
    return (update.T, inverse)


def solution(mesh):
    placed = (
        P(None, ("groups", "dp")),
        P(None, ("groups", "dp")),
        P(("groups", "dp")),
        P(("groups", "dp")),
        P("groups"),
        P("groups", None),
        P("groups"),
        P("groups", None),
        P("groups"),
        P("groups", None),
        P("groups"),
    )
    return jax.shard_map(
        on_device,
        mesh=mesh,
        in_specs=placed,
        out_specs=(P(("groups", "dp"), None), P(("groups", "dp"), None)),
        check_vma=False,
    )
```
